1024 devices in a mesh: seq: 16 (over x_hi, z), exp: 4 (over x_lo), ffn: 16 (over y, core).
Axes of the slice: x: 8 (x_hi: 2, x_lo: 4; x = x_hi * 4 + x_lo), y: 8, z: 8, core: 2. Of those that a mesh axis runs over, the one named last changes fastest.
Arguments:
- tokens: bfloat16 [4096, 3072], P(('seq', 'exp')), may hold values from -6 to 6
- cotangent: bfloat16 [4096, 3072], P(('seq', 'exp')), may hold values from -1.5 to 1.5
- routes: int32 [4096, 2], P(('seq', 'exp')), may hold values from 0 to 3, all different within a row; in each aligned block of 64 rows (0 to 63, 64 to 127, ...) at most 36 rows name the same one
- router_gates: float32 [4096, 2], P(('seq', 'exp')), may hold values from 0.1 to 1
- gate_weight: bfloat16 [4, 3072, 5376], P('exp', None, 'ffn'), may hold values from -0.109375 to 0.109375
- up_weight: bfloat16 [4, 3072, 5376], P('exp', None, 'ffn'), may hold values from -0.109375 to 0.109375
- down_weight: bfloat16 [4, 5376, 3072], P('exp', 'ffn'), may hold values from -0.078125 to 0.078125
Outputs:
- layer_out: bfloat16 [4096, 3072], P(('seq', 'exp'), 'ffn')
- token_grad: bfloat16 [4096, 3072], P(('seq', 'exp'), 'ffn')
- gate_weight_grad: float32 [4, 3072, 5376], P('exp', 'seq', 'ffn')
- up_weight_grad: float32 [4, 3072, 5376], P('exp', 'seq', 'ffn')
- down_weight_grad: float32 [4, 5376, 3072], P('exp', 'ffn', 'seq')
The draws below stay inside these ranges and needn't reach their ends.
Inputs may be any that keep to these rules, and one draw needn't show every extreme that they name: `routes`: among the 64 rows of one device no expert is named by more than 36 rows, and some device has an expert named by exactly 36 of its rows.
All inputs are finite; a program needn't handle non-finite values.
Results may differ from the reference program's by a relative error of at most 0.024.
Values may be sent and summed in bfloat16 or wider, within the bound.
No kernel may reach another device: no remote copies, remote signals or barrier semaphores. Data moves between devices by JAX's collectives and lax.ppermute only.
A program may use at most 64 MiB of HBM per device.

```python
import math
import jax
import jax.numpy as jnp
import numpy as np
from jax import lax

D = 3072
FF = 5376
EXPERTS = 4
TOPK = 2
TOK_DEV = 64
CAP = 36
TOKENS = 4096
N_SEQ = 16
N_EXP = 4
N_FFN = 16


def block_scale(own_key, dims, cuts, low, top_value):
    level, own = 1.0, jax.random.fold_in(own_key, 6)
    for axis_at, shards_of in cuts:
        heights = jnp.exp(jax.random.uniform(jax.random.fold_in(own, axis_at), (shards_of,), jnp.float32, low / len(cuts), top_value / len(cuts)))
        level = level * jnp.repeat(heights, dims[axis_at] // shards_of).reshape([-1 if axis == axis_at else 1 for axis in range(len(dims))])
    return level


def deal_out(key, own, number, rows, amount, top, bound, lean):
    order = jax.random.permutation(key, amount)
    crowded, usual = load_shares(amount, rows * top, bound, lean, True), load_shares(amount, rows * top, bound, lean, False)
    places = jnp.arange(amount)

    def named(sizes, offset_by):
        used = int((sizes > 0).sum())
        fixed = max(1, used // 4)
        moved = fixed + (places - fixed + offset_by * (used - fixed)) % max(1, amount - fixed)
        return jnp.zeros((amount,), jnp.int32).at[order[jnp.where(places < fixed, places, moved)]].set(jnp.asarray(sizes, jnp.int32))

    sizes = jnp.where(number % 4 == 0, named(crowded, number // 4), named(usual, number - number // 4 - 1))
    mixed = jax.random.permutation(jax.random.fold_in(own, 3), amount)
    giver, sink = mixed[0:amount // 2 * 2:2], mixed[1:amount // 2 * 2:2]
    slack = jnp.minimum(sizes[giver] - 1, bound - sizes[sink]) // 2
    slack = jnp.where((giver == order[0]) | (sink == order[0]) | (sizes[sink] == 0), 0, jnp.maximum(slack, 0))
    moved = jax.random.randint(jax.random.fold_in(own, 4), (amount // 2,), 0, 1 << 20) % (slack + 1)
    sizes = sizes.at[giver].add(-moved).at[sink].add(moved)
    members = jnp.searchsorted(jnp.cumsum(sizes), jnp.arange(rows * top), side="right").astype(jnp.int32)
    listing = members.reshape(top, rows).T
    listing = listing[jax.random.permutation(jax.random.fold_in(own, 1), rows)]
    offset_by = jax.random.randint(jax.random.fold_in(own, 2), (rows, 1), 0, top)
    return jnp.take_along_axis(listing, (jnp.arange(top)[None, :] + offset_by) % top, axis=1)


def load_shares(count, total, most, skew, full):
    portions = [(1 << 20) // math.isqrt(rank ** skew) + 1 for rank in range(1, count + 1)]
    largest = most if full else min(most, max(-(-total // count), total * portions[0] // sum(portions)))
    least = 1 if total - largest >= count - 1 else 0
    holding, spare = [largest] + [least] * (count - 1), total - largest - least * (count - 1)
    while spare > 0:
        free = [i for i in range(1, count) if holding[i] < largest] or [i for i in range(1, count) if holding[i] < most]
        mass, budget = sum([portions[i] for i in free]), spare
        for i in free:
            addition = min(most - holding[i], max(1, budget * portions[i] // mass), spare)
            holding[i] = holding[i] + addition
            spare = spare - addition
    return np.array(holding)


def centred(own_key, dims, scale, most, cuts=(), kind=jnp.bfloat16):
    values = scale * jax.random.normal(own_key, dims, jnp.float32)
    if cuts:
        values = values * block_scale(own_key, dims, cuts, -0.22, 0.18)
    return jnp.clip(values, -most, most).astype(kind)


def setup_inputs(seed: int = 0) -> dict:
    key_of = jax.random.split(jax.random.key(seed), 8)
    tokens = centred(key_of[0], (TOKENS, D), 1.0, 6.0, ((0, 64),))
    cotangent = centred(key_of[1], (TOKENS, D), 0.25, 1.5, ((0, 64),))
    routes_keys = jax.random.split(jax.random.fold_in(key_of[2], 1), TOKENS // TOK_DEV)
    routes_turns = jax.random.permutation(jax.random.fold_in(key_of[2], 3), TOKENS // TOK_DEV)
    routes = jax.vmap(lambda own, number: deal_out(jax.random.fold_in(key_of[2], 2), own, number, TOK_DEV, EXPERTS, TOPK, CAP, 2))(routes_keys, routes_turns).reshape((TOKENS, TOPK))
    router_gates = jnp.clip(0.1 + 0.9 * jax.random.uniform(key_of[3], (TOKENS, TOPK), jnp.float32) ** block_scale(key_of[3], (TOKENS, TOPK), ((0, 64),), -0.2, 0.2), 0.1, 1.0)
    gate_weight = centred(key_of[4], (EXPERTS, D, FF), D ** -0.5, 0.109375, ((0, 4), (2, 16)))
    up_weight = centred(key_of[5], (EXPERTS, D, FF), D ** -0.5, 0.109375, ((0, 4), (2, 16)))
    down_weight = centred(key_of[6], (EXPERTS, FF, D), FF ** -0.5, 0.078125, ((0, 4), (1, 16)))
    return {"tokens": tokens, "cotangent": cotangent, "routes": routes, "router_gates": router_gates, "gate_weight": gate_weight, "up_weight": up_weight, "down_weight": down_weight}


highest = lax.Precision.HIGHEST


def rounded(value):
    return lax.optimization_barrier(value.astype(jnp.bfloat16)).astype(jnp.float32)


def reference(tokens, cotangent, routes, router_gates, gate_weight, up_weight, down_weight):
    group_size = TOKENS // N_SEQ
    capacity_rows = N_EXP * CAP
    block_width = FF // N_FFN
    gate_full = gate_weight.astype(jnp.float32)
    up_full = up_weight.astype(jnp.float32)
    down_full = down_weight.astype(jnp.float32)
    scaled = (router_gates[:, :, None] * cotangent.astype(jnp.float32)[:, None, :]).astype(jnp.bfloat16)
    tokens_grouped = tokens.astype(jnp.float32).reshape(N_SEQ, group_size, D)
    scaled_grouped = scaled.astype(jnp.float32).reshape(N_SEQ, group_size * TOPK, D)
    routes_grouped = routes.reshape(N_SEQ, group_size * TOPK)
    gates_grouped = router_gates.reshape(N_SEQ, group_size * TOPK)

    def one_group(carry, inputs):
        grads_gate, grads_up, grads_down = carry
        x_group, dy_group, id_group, gate_group = inputs
        out_group = jnp.zeros((group_size, D), jnp.float32)
        back_group = jnp.zeros((group_size, D), jnp.float32)
        for expert in range(EXPERTS):
            match_flags = id_group == expert
            order = jnp.argsort(jnp.where(match_flags, 0, 1).astype(jnp.int32), stable=True)[:capacity_rows]
            order = order.astype(jnp.int32)
            live = match_flags[order].astype(jnp.float32)
            token_index = (order // TOPK).astype(jnp.int32)
            rows_x = x_group[token_index] * live[:, None]
            rows_dy = dy_group[order] * live[:, None]
            gate_act = jnp.dot(rows_x, gate_full[expert], precision=highest)
            up_act = jnp.dot(rows_x, up_full[expert], precision=highest)
            sigmoid_gate = jax.nn.sigmoid(gate_act)
            hidden = rounded(gate_act * sigmoid_gate * up_act)
            out_blocks = jnp.einsum("rnf,nfd->nrd", hidden.reshape(capacity_rows, N_FFN, block_width),
                                    down_full[expert].reshape(N_FFN, block_width, D), precision=highest)
            expert_out = rounded(jnp.sum(rounded(out_blocks), axis=0))
            hidden_grad = jnp.dot(rows_dy, down_full[expert].T, precision=highest)
            gate_grad = rounded(hidden_grad * up_act * sigmoid_gate * (1.0 + gate_act * (1.0 - sigmoid_gate)))
            up_grad = rounded(hidden_grad * gate_act * sigmoid_gate)
            back_blocks = jnp.einsum("rnf,dnf->nrd", gate_grad.reshape(capacity_rows, N_FFN, block_width),
                                     gate_full[expert].reshape(D, N_FFN, block_width), precision=highest)
            back_blocks = back_blocks + jnp.einsum("rnf,dnf->nrd", up_grad.reshape(capacity_rows, N_FFN, block_width),
                                                   up_full[expert].reshape(D, N_FFN, block_width), precision=highest)
            expert_back = rounded(jnp.sum(rounded(back_blocks), axis=0))
            weights_now = gate_group[order] * live
            out_group = out_group.at[token_index].add(weights_now[:, None] * expert_out)
            back_group = back_group.at[token_index].add(live[:, None] * expert_back)
            grads_gate = grads_gate.at[expert].add(rounded(jnp.dot(rows_x.T, gate_grad, precision=highest)))
            grads_up = grads_up.at[expert].add(rounded(jnp.dot(rows_x.T, up_grad, precision=highest)))
            grads_down = grads_down.at[expert].add(rounded(jnp.dot(hidden.T, rows_dy, precision=highest)))
        return (grads_gate, grads_up, grads_down), (out_group, back_group)

    start = (jnp.zeros((EXPERTS, D, FF), jnp.float32), jnp.zeros((EXPERTS, D, FF), jnp.float32),
             jnp.zeros((EXPERTS, FF, D), jnp.float32))
    grads, outputs = lax.scan(one_group, start, (tokens_grouped, scaled_grouped, routes_grouped, gates_grouped))
    layer_out = outputs[0].reshape(TOKENS, D).astype(jnp.bfloat16)
    token_grad = outputs[1].reshape(TOKENS, D).astype(jnp.bfloat16)
    return (layer_out, token_grad, grads[0], grads[1], grads[2])
```

```python
import functools

import jax
import jax.numpy as jnp
from jax import lax
from jax.experimental import pallas as pl
from jax.experimental.pallas import tpu as pltpu
from jax.sharding import Mesh, PartitionSpec as P

CAP = 36
SLOT = 40
N_Z = 8
N_Y = 8
N_XL = 4
BF16 = jnp.bfloat16
F32 = jnp.float32
HIGHEST = lax.Precision.HIGHEST


def dot(a, b, dims=((1,), (0,)), precision=None):
    return lax.dot_general(a, b, (dims, ((), ())), precision=precision, preferred_element_type=F32)


def picks(routes, gates):
    tok_count = routes.shape[1]
    shape = (N_XL * SLOT, tok_count)
    row = lax.broadcasted_iota(jnp.int32, shape, 0)
    expert = sum((row >= SLOT * i).astype(jnp.int32) for i in range(1, N_XL))
    slot = (row - SLOT * expert).astype(F32)
    first = routes[0:1, :] == expert
    second = routes[1:2, :] == expert
    member = jnp.where(first | second, 1.0, 0.0).astype(F32)
    at = lax.broadcasted_iota(jnp.int32, (tok_count, tok_count), 0)
    to = lax.broadcasted_iota(jnp.int32, (tok_count, tok_count), 1)
    earlier = jnp.where(at < to, 1.0, 0.0).astype(BF16)
    rank = dot(member.astype(BF16), earlier)
    pick = jnp.where(rank == slot, member, 0.0)
    gate = jnp.where(first, gates[0:1, :], gates[1:2, :]) * pick
    return pick, gate


def squeeze_matrix(rows, slots):
    row = lax.broadcasted_iota(jnp.int32, (rows, slots), 0)
    col = lax.broadcasted_iota(jnp.int32, (rows, slots), 1)
    expert = sum((row >= CAP * i).astype(jnp.int32) for i in range(1, N_XL))
    return jnp.where(col == row + (SLOT - CAP) * expert, 1.0, 0.0).astype(BF16)


def dispatch(flags, routes, gates, tokens, cotangent, rows_out):
    pick, gate = picks(routes[...], gates[...])
    pick = pick.astype(BF16)

    @pl.when(flags[0] == 0)
    def _():
        rows_out[...] = dot(pick, tokens[...]).astype(BF16)

    @pl.when(flags[0] != 0)
    def _():
        scale = jnp.sum(gate, axis=1, keepdims=True)
        rows_out[...] = (dot(pick, cotangent[...]) * scale).astype(BF16)


def squeeze(flags, rows, full_out, cols_out):
    count = full_out.shape[0]
    full = dot(squeeze_matrix(count, rows.shape[0]), rows[...]).astype(BF16)
    full_out[...] = full
    width = full.shape[1]
    half = width // 2
    part = half // N_Z

    def write(swap):
        for i in range(N_Z):
            low = full[:, part * i : part * (i + 1)]
            high = full[:, half + part * i : half + part * (i + 1)]
            pair = [high, low] if swap else [low, high]
            cols_out[i] = jnp.concatenate(pair, axis=1)

    @pl.when(flags[1] == 0)
    def _():
        write(False)

    @pl.when(flags[1] != 0)
    def _():
        write(True)


def expert_front(flags, mine, other, gate_w, up_w, down_w, pieces_out):
    is_x = flags[0] == 0
    a, b = mine[...], other[...]
    x = jnp.where(is_x, a, b)
    dy = jnp.where(is_x, b, a)
    gate_act = dot(x, gate_w[0])
    up_act = dot(x, up_w[0])
    hidden_grad = dot(dy, down_w[0], ((1,), (1,)))
    s = 1.0 / (1.0 + jnp.exp(-gate_act))
    silu = gate_act * s
    hidden = (silu * up_act).astype(BF16)
    gate_grad = (hidden_grad * up_act * s * (1.0 + gate_act * (1.0 - s))).astype(BF16)
    up_grad = (hidden_grad * silu).astype(BF16)
    pieces_out[...] = jnp.concatenate([hidden, gate_grad, up_grad], axis=1)


def expert_back(flags, pieces, gate_w, up_w, down_w, keep_out, send_out):
    ff = pieces.shape[1] // 3
    hidden = pieces[:, :ff]
    gate_grad = pieces[:, ff : 2 * ff]
    up_grad = pieces[:, 2 * ff :]
    out = dot(hidden, down_w[0]).astype(BF16)
    back = dot(gate_grad, gate_w[0], ((1,), (1,))) + dot(up_grad, up_w[0], ((1,), (1,)))
    back = back.astype(BF16)
    part = out.shape[1] // (2 * N_Y)

    def write(even, odd):
        for i in range(N_Y):
            for j, ref in ((2 * i, even), (2 * i + 1, odd)):
                at = slice(part * j, part * (j + 1))
                ref[i] = jnp.concatenate([out[:, at], back[:, at]], axis=1)

    @pl.when(flags[0] == 0)
    def _():
        write(keep_out, send_out)

    @pl.when(flags[0] != 0)
    def _():
        write(send_out, keep_out)


def add_up(blocks, rows_out):
    total = blocks[0].astype(F32)
    for i in range(1, N_Y):
        total = total + blocks[i].astype(F32)
    count = total.shape[0]
    spread = squeeze_matrix(count, rows_out.shape[0])
    rows_out[...] = dot(spread, total.astype(BF16), ((0,), (0,))).astype(BF16)


def combine(routes, gates, rows, layer_out, grad_out):
    pick, gate = picks(routes[...], gates[...])
    part = layer_out.shape[1]
    both = rows[...]
    layer_out[...] = dot(gate, both[:, :part].astype(F32), ((0,), (0,)), HIGHEST).astype(BF16)
    grad_out[...] = dot(pick.astype(BF16), both[:, part:], ((0,), (0,))).astype(BF16)


def weight_grads(flags, pieces, mine, other, keep_out, send_out):
    is_x = flags[0] == 0
    a, b = mine[...], other[...]
    x = jnp.where(is_x, a, b)
    dy = jnp.where(is_x, b, a)
    ff = pieces.shape[1] // 3
    down = dot(dy, pieces[:, :ff], ((0,), (0,)))
    gate_up = dot(x, pieces[:, ff:], ((0,), (0,)))
    part = keep_out.shape[0]
    both = jnp.concatenate([down, gate_up], axis=1)
    keep_out[...] = both[:part]
    send_out[...] = both[part:].astype(BF16)


def finish(keep, got, gate_out, up_out, down_out):
    total = keep[...] + got[...].astype(F32)
    ff = total.shape[1] // 3
    down_out[0] = total[:, :ff].T
    gate_out[0] = total[:, ff : 2 * ff]
    up_out[0] = total[:, 2 * ff :]


def call(body, outs, scalars, *operands):
    vmem = pl.BlockSpec(memory_space=pltpu.VMEM)
    specs = [pl.BlockSpec(memory_space=pltpu.SMEM)] * len(scalars) + [vmem] * len(operands)
    return pl.pallas_call(
        body,
        out_shape=[jax.ShapeDtypeStruct(s, t) for s, t in outs],
        in_specs=specs,
        out_specs=[vmem] * len(outs),
        compiler_params=pltpu.CompilerParams(vmem_limit_bytes=40 * 1024 * 1024),
        name=body.__name__,
    )(*scalars, *operands)


def swap(value, axis):
    return lax.ppermute(value, axis, [(0, 1), (1, 0)])


def on_device(tokens, cotangent, routes, router_gates, gate_weight, up_weight, down_weight):
    width = tokens.shape[1]
    tok_count = tokens.shape[0]
    ff = gate_weight.shape[2]
    part = width // 16
    slots = N_XL * SLOT
    rows = N_XL * CAP
    flags = jnp.stack([lax.axis_index("c"), lax.axis_index("xh")]).astype(jnp.int32)
    routes = routes.T
    gates = router_gates.T

    (sent,) = call(dispatch, [((slots, width), BF16)], [flags], routes, gates, tokens, cotangent)
    got = lax.all_to_all(
        sent.reshape(N_XL, SLOT, width), "xl", split_axis=0, concat_axis=0, tiled=True
    ).reshape(slots, width)
    mine, cols = call(
        squeeze, [((rows, width), BF16), ((N_Z, rows, 2 * part), BF16)], [flags], got
    )
    other = swap(mine, "c")
    (pieces,) = call(
        expert_front,
        [((rows, 3 * ff), BF16)],
        [flags],
        mine,
        other,
        gate_weight,
        up_weight,
        down_weight,
    )
    cols = lax.all_to_all(cols, "z", split_axis=0, concat_axis=0, tiled=True)
    cols = cols.reshape(N_Z * rows, 2 * part)
    cols_other = swap(cols, "c")
    pieces_all = lax.all_gather(pieces, "z", axis=0, tiled=True)

    keep, send = call(
        expert_back,
        [((N_Y, rows, 2 * part), BF16)] * 2,
        [flags],
        pieces,
        gate_weight,
        up_weight,
        down_weight,
    )
    summed = (keep.astype(F32) + swap(send, "c").astype(F32)).astype(BF16)
    blocks = lax.all_to_all(summed, "y", split_axis=0, concat_axis=0, tiled=True)
    (back,) = call(add_up, [((slots, 2 * part), BF16)], [], blocks)
    back = lax.all_to_all(
        back.reshape(N_XL, SLOT, 2 * part), "xl", split_axis=0, concat_axis=0, tiled=True
    ).reshape(slots, 2 * part)
    layer_out, token_grad = call(
        combine, [((tok_count, part), BF16)] * 2, [], routes, gates, back
    )

    kept, given = call(
        weight_grads,
        [((part, 3 * ff), F32), ((part, 3 * ff), BF16)],
        [flags],
        pieces_all,
        cols,
        cols_other,
    )
    grad_gate, grad_up, grad_down = call(
        finish,
        [((1, part, ff), F32), ((1, part, ff), F32), ((1, ff, part), F32)],
        [],
        kept,
        swap(given, "xh"),
    )
    return layer_out, token_grad, grad_gate, grad_up, grad_down


def solution(mesh):
    fine = Mesh(
        mesh.devices.reshape(2, N_Z, N_XL, N_Y, 2), ("xh", "z", "xl", "y", "c")
    )
    seq, ffn = ("xh", "z"), ("y", "c")
    rows = P(("xh", "z", "xl"), None)
    return jax.shard_map(
        on_device,
        mesh=fine,
        in_specs=(
            rows,
            rows,
            rows,
            rows,
            P("xl", None, ffn),
            P("xl", None, ffn),
            P("xl", ffn, None),
        ),
        out_specs=(
            P(("xh", "z", "xl"), ffn),
            P(("xh", "z", "xl"), ffn),
            P("xl", seq, ffn),
            P("xl", seq, ffn),
            P("xl", ffn, seq),
        ),
        check_vma=False,
    )
```

```python
import jax
import jax.numpy as jnp
from jax import lax
from jax.experimental import pallas as pl
from jax.experimental.pallas import tpu as pltpu
from jax.sharding import Mesh, PartitionSpec as P

CAP = 36
SLOT = 40
SOON = (0, 1, 7, 2, 6, 3, 5)
CUTS = 3
N_Z = 8
N_Y = 8
N_XL = 4
VMEM_BYTES = 20 * 1024 * 1024
BF16 = jnp.bfloat16
F32 = jnp.float32
HIGHEST = lax.Precision.HIGHEST


def dot(a, b, dims=((1,), (0,)), precision=None):
    return lax.dot_general(a, b, (dims, ((), ())), precision=precision, preferred_element_type=F32)


def picks(routes, gates, base=0):
    tok_count = routes.shape[1]
    shape = (N_XL * SLOT, tok_count)
    row = lax.broadcasted_iota(jnp.int32, shape, 0)
    expert = sum((row >= SLOT * i).astype(jnp.int32) for i in range(1, N_XL))
    slot = (row - SLOT * expert).astype(F32)
    expert = expert + base
    expert = jnp.where(expert >= N_XL, expert - N_XL, expert)
    first = routes[0:1, :] == expert
    second = routes[1:2, :] == expert
    member = jnp.where(first | second, 1.0, 0.0).astype(F32)
    at = lax.broadcasted_iota(jnp.int32, (tok_count, tok_count), 0)
    to = lax.broadcasted_iota(jnp.int32, (tok_count, tok_count), 1)
    earlier = jnp.where(at < to, 1.0, 0.0).astype(BF16)
    rank = dot(member.astype(BF16), earlier)
    pick = jnp.where(rank == slot, member, 0.0)
    gate = jnp.where(first, gates[0:1, :], gates[1:2, :]) * pick
    return pick, gate


def squeeze_matrix(rows, slots):
    row = lax.broadcasted_iota(jnp.int32, (rows, slots), 0)
    col = lax.broadcasted_iota(jnp.int32, (rows, slots), 1)
    expert = sum((row >= CAP * i).astype(jnp.int32) for i in range(1, N_XL))
    return jnp.where(col == row + (SLOT - CAP) * expert, 1.0, 0.0).astype(BF16)


def fetch_rows(pairs, sems):
    cuts = []
    for i, (a, b) in enumerate(pairs):
        step = a.shape[1] // CUTS
        at = [pl.ds(step * k, step) for k in range(CUTS)]
        cuts.append([pltpu.make_async_copy(a.at[:, r], b.at[:, r], sems.at[CUTS * i + k]) for k, r in enumerate(at)])
    for group in cuts:
        for copy in group:
            copy.start()
    return cuts


def fetch(pairs, sems):
    copies = [pltpu.make_async_copy(a, b, sems.at[i]) for i, (a, b) in enumerate(pairs)]
    for copy in copies:
        copy.start()
    return copies


def wait_all(copies):
    for copy in copies:
        copy.wait()


def dispatch(flags, routes_at, gates_at, tokens, cotangent, *refs):
    rows_out, (routes, gates, source, sem, sems) = refs[:N_XL], refs[N_XL:]
    is_x = flags[0] == 0
    copies = fetch(((routes_at, routes), (gates_at, gates)), sems)

    @pl.when(is_x)
    def _():
        pltpu.make_async_copy(tokens, source, sem).start()

    @pl.when(jnp.logical_not(is_x))
    def _():
        pltpu.make_async_copy(cotangent, source, sem).start()

    for copy in copies:
        copy.wait()
    pick, gate = picks(routes[...], gates[...], flags[3])
    scale = jnp.where(is_x, 1.0, jnp.sum(gate, axis=1, keepdims=True))
    pltpu.make_async_copy(tokens, source, sem).wait()
    rows = (dot(pick.astype(BF16), source[...]) * scale).astype(BF16)
    for k in range(N_XL):
        rows_out[k][...] = rows[SLOT * k : SLOT * (k + 1)]


def squeeze(flags, *refs):
    parts, (full_out, cols_out, cols, sems) = refs[:N_XL], refs[N_XL:]
    rows = jnp.concatenate([part[...] for part in parts], axis=0)
    matrix = squeeze_matrix(full_out.shape[0], rows.shape[0])
    full = dot(matrix, rows).astype(BF16)
    full_out[...] = full
    half = full.shape[1] // 2
    part = half // N_Z

    def write(swapped):
        for i in range(N_Z):
            low = full[:, part * i : part * (i + 1)]
            high = full[:, half + part * i : half + part * (i + 1)]
            cols[i] = jnp.concatenate([high, low] if swapped else [low, high], axis=1)

    @pl.when(flags[1] == 0)
    def _():
        write(False)

    @pl.when(flags[1] != 0)
    def _():
        write(True)

    wait_all(fetch([(cols.at[i], cols_out.at[i]) for i in range(N_Z)], sems))


def expert_front(flags, mine, other, gate_w, up_w, down_w, pieces_out, gate_v, up_v, down_v, sems):
    copies = fetch_rows(((gate_w, gate_v), (up_w, up_v), (down_w, down_v)), sems)
    is_x = flags[0] == 0
    a, b = mine[...], other[...]
    x = jnp.where(is_x, a, b)
    dy = jnp.where(is_x, b, a)
    wait_all(copies[0])
    gate_act = dot(x, gate_v[0], ((1,), (1,)))
    wait_all(copies[1])
    up_act = dot(x, up_v[0], ((1,), (1,)))
    wait_all(copies[2])
    hidden_grad = dot(dy, down_v[0], ((1,), (1,)))
    s = 1.0 / (1.0 + jnp.exp(-gate_act))
    silu = gate_act * s
    hidden = (silu * up_act).astype(BF16)
    gate_grad = (hidden_grad * up_act * s * (1.0 + gate_act * (1.0 - s))).astype(BF16)
    up_grad = (hidden_grad * silu).astype(BF16)
    pieces_out[...] = jnp.concatenate([hidden, gate_grad, up_grad], axis=1)


def expert_back(
    flags, pieces, gate_w, up_w, down_w, keep_out, send_out, gate_v, up_v, down_v, sems
):
    copies = fetch_rows(((down_w, down_v), (gate_w, gate_v), (up_w, up_v)), sems)
    ff = pieces.shape[1] // 3
    hidden = pieces[:, :ff]
    gate_grad = pieces[:, ff : 2 * ff]
    up_grad = pieces[:, 2 * ff :]
    wait_all(copies[0])
    out = dot(hidden, down_v[0]).astype(BF16)
    wait_all(copies[1])
    wait_all(copies[2])
    back = (dot(gate_grad, gate_v[0]) + dot(up_grad, up_v[0])).astype(BF16)
    part = out.shape[1] // (2 * N_Y)

    def write(even, odd):
        for i in range(N_Y):
            for j, ref in ((2 * i, even), (2 * i + 1, odd)):
                at = slice(part * j, part * (j + 1))
                ref[i] = jnp.concatenate([out[:, at], back[:, at]], axis=1)

    @pl.when(flags[0] == 0)
    def _():
        write(keep_out, send_out)

    @pl.when(flags[0] != 0)
    def _():
        write(send_out, keep_out)


def add_up(flags, blocks, rows_out):
    total = blocks[0].astype(F32)
    for i in range(1, N_Y):
        total = total + blocks[i].astype(F32)
    spread_out = squeeze_matrix(total.shape[0], N_XL * SLOT)
    rows = dot(spread_out, total.astype(BF16), ((0,), (0,))).astype(BF16)
    for k in range(N_XL):
        rows_out[lax.rem(flags[3] + (N_XL - k), N_XL)] = rows[SLOT * k : SLOT * (k + 1)]


def combine(routes, gates, rows, layer_out, grad_out):
    pick, gate = picks(routes[...], gates[...])
    part = layer_out.shape[1]
    both = rows[...]
    layer_out[...] = dot(gate, both[:, :part].astype(F32), ((0,), (0,)), HIGHEST).astype(BF16)
    grad_out[...] = dot(pick.astype(BF16), both[:, part:], ((0,), (0,))).astype(BF16)


def grads_of(flags, mine, other, distances, rows):
    is_x = flags[0] == 0
    order = [lax.rem(flags[2] + (N_Z - k), N_Z) for k in distances]
    a = jnp.concatenate([mine[k] for k in order], axis=0)
    b = jnp.concatenate([other[k] for k in order], axis=0)
    x = jnp.where(is_x, a, b)
    dy = jnp.where(is_x, b, a)
    ff = rows.shape[1] // 3
    down = dot(dy, rows[:, :ff], ((0,), (0,)))
    gate_up = dot(x, rows[:, ff:], ((0,), (0,)))
    return jnp.concatenate([down, gate_up], axis=1)


def weight_grads(flags, mine, other, *refs):
    *pieces, total_out, held, sems = refs
    count = pieces[0].shape[0]
    places = [held.at[pl.ds(count * i, count)] for i in range(len(SOON))]
    wait_all(fetch(list(zip(pieces, places)), sems))
    total_out[...] = grads_of(flags, mine, other, SOON, held[...])


def weight_grads_last(flags, mine, other, piece, total, keep_out, send_out):
    both = total[...] + grads_of(flags, mine, other, (N_Z // 2,), piece[...])
    part = keep_out.shape[0]
    keep_out[...] = both[:part]
    send_out[...] = both[part:].astype(BF16)


def finish(keep, got, gate_out, up_out, down_out):
    total = keep[...] + got[...].astype(F32)
    ff = total.shape[1] // 3
    down_out[0] = total[:, :ff]
    gate_out[0] = total[:, ff : 2 * ff]
    up_out[0] = total[:, 2 * ff :]


def call(body, outs, scalars, *operands, far=(), scratch=(), flops=0, far_outs=0):
    vmem = pl.BlockSpec(memory_space=pltpu.VMEM)
    smem = pl.BlockSpec(memory_space=pltpu.SMEM)
    hbm = pl.BlockSpec(memory_space=pltpu.HBM)
    moved = sum(v.size * v.dtype.itemsize for v in (*operands, *far))
    cost = pl.CostEstimate(flops=flops, transcendentals=0, bytes_accessed=moved)
    return pl.pallas_call(
        body,
        out_shape=[
            jax.ShapeDtypeStruct(s, t) if i < len(outs) - far_outs else pltpu.HBM(s, t)
            for i, (s, t) in enumerate(outs)
        ],
        in_specs=[smem] * len(scalars)
        + [vmem] * len(operands)
        + [hbm] * len(far),
        out_specs=[vmem] * (len(outs) - far_outs) + [hbm] * far_outs,
        scratch_shapes=list(scratch),
        compiler_params=pltpu.CompilerParams(vmem_limit_bytes=VMEM_BYTES),
        cost_estimate=cost if flops else None,
        name=body.__name__,
    )(*scalars, *operands, *[pltpu.with_memory_space_constraint(v, pltpu.HBM) for v in far])


def shift(value, by):
    return lax.ppermute(value, "z", [(i, (i + by) % N_Z) for i in range(N_Z)])


def spread(parts, axis, forward=1):
    count = len(parts)
    return [parts[0]] + [
        lax.ppermute(parts[k], axis, [(i, (i + forward * k) % count) for i in range(count)])
        for k in range(1, count)
    ]


def swap(value, axis):
    return lax.ppermute(value, axis, [(0, 1), (1, 0)])


def on_device(tokens, cotangent, routes, router_gates, gate_weight, up_weight, down_weight):
    width = tokens.shape[1]
    tok_count = tokens.shape[0]
    ff = gate_weight.shape[2]
    part = width // 16
    slots = N_XL * SLOT
    rows = N_XL * CAP
    work = 3 * 2 * rows * width * ff
    flags = jnp.stack([lax.axis_index(a) for a in ("c", "xh", "z", "xl", "y")]).astype(jnp.int32)
    routes = routes.T
    gates = router_gates.T
    weights = (jnp.swapaxes(gate_weight, 1, 2), jnp.swapaxes(up_weight, 1, 2), down_weight)
    held = [pltpu.VMEM(w.shape, BF16) for w in weights]
    held.append(pltpu.SemaphoreType.DMA((3 * CUTS,)))

    sent = call(
        dispatch,
        [((SLOT, width), BF16)] * N_XL,
        [flags],
        far=(routes, gates, tokens, cotangent),
        scratch=(
            pltpu.VMEM(routes.shape, routes.dtype),
            pltpu.VMEM(gates.shape, gates.dtype),
            pltpu.VMEM(tokens.shape, BF16),
            pltpu.SemaphoreType.DMA,
            pltpu.SemaphoreType.DMA((2,)),
        ),
    )
    got = spread(sent, "xl")
    mine, cols = call(
        squeeze,
        [((rows, width), BF16), ((N_Z, rows, 2 * part), BF16)],
        [flags],
        *got,
        scratch=(pltpu.VMEM((N_Z, rows, 2 * part), BF16), pltpu.SemaphoreType.DMA((N_Z,))),
        far_outs=1,
    )
    other = swap(mine, "c")
    cols = lax.all_to_all(cols, "z", split_axis=0, concat_axis=0, tiled=True)
    (pieces,) = call(
        expert_front, [((rows, 3 * ff), BF16)], [flags], mine, other, far=weights, scratch=held
    )
    keep, send = call(
        expert_back,
        [((N_Y, rows, 2 * part), BF16)] * 2,
        [flags],
        pieces,
        far=weights,
        scratch=held,
        flops=work,
    )
    summed = (keep.astype(F32) + swap(send, "c").astype(F32)).astype(BF16)

    found = [pieces] + [None] * (N_Z - 1)
    for k in range(1, N_Z // 2):
        found[k] = shift(found[k - 1], 1)
        found[N_Z - k] = shift(found[(N_Z - k + 1) % N_Z], -1)
    found[N_Z // 2] = shift(found[N_Z // 2 - 1], 1)
    cols_other = swap(cols, "c")

    blocks = lax.all_to_all(summed, "y", split_axis=0, concat_axis=0, tiled=True)
    (back,) = call(add_up, [((N_XL, SLOT, 2 * part), BF16)], [flags], blocks)
    back = lax.all_to_all(back, "xl", split_axis=0, concat_axis=0, tiled=True)
    layer_out, token_grad = call(
        combine,
        [((tok_count, part), BF16)] * 2,
        [],
        routes,
        gates,
        back.reshape(slots, 2 * part),
    )

    (total,) = call(
        weight_grads,
        [((2 * part, 3 * ff), F32)],
        [flags],
        cols,
        cols_other,
        far=[found[k] for k in SOON],
        scratch=(
            pltpu.VMEM((len(SOON) * rows, 3 * ff), BF16),
            pltpu.SemaphoreType.DMA((len(SOON),)),
        ),
        flops=2 * len(SOON) * rows * 2 * part * 3 * ff,
    )
    kept, given = call(
        weight_grads_last,
        [((part, 3 * ff), F32), ((part, 3 * ff), BF16)],
        [flags],
        cols,
        cols_other,
        found[N_Z // 2],
        total,
    )
    grad_gate, grad_up, grad_down = call(
        finish, [((1, part, ff), F32)] * 3, [], kept, swap(given, "xh")
    )
    return layer_out, token_grad, grad_gate, grad_up, jnp.swapaxes(grad_down, 1, 2)


def solution(mesh):
    fine = Mesh(
        mesh.devices.reshape(2, N_Z, N_XL, N_Y, 2), ("xh", "z", "xl", "y", "c")
    )
    seq, ffn = ("xh", "z"), ("y", "c")
    rows = P(("xh", "z", "xl"), None)
    return jax.shard_map(
        on_device,
        mesh=fine,
        in_specs=(
            rows,
            rows,
            rows,
            rows,
            P("xl", None, ffn),
            P("xl", None, ffn),
            P("xl", ffn, None),
        ),
        out_specs=(
            P(("xh", "z", "xl"), ffn),
            P(("xh", "z", "xl"), ffn),
            P("xl", seq, ffn),
            P("xl", seq, ffn),
            P("xl", ffn, seq),
        ),
        check_vma=False,
    )
```

```python
import jax
import jax.numpy as jnp
from jax import lax
from jax.experimental import pallas as pl
from jax.experimental.pallas import tpu as pltpu
from jax.sharding import Mesh, PartitionSpec as P

CAP = 36
SLOT = 40
SOON = (0, 1, 7, 2, 6, 3)
LAST = (5, 4)
CUTS = 3
N_Z = 8
N_Y = 8
N_XL = 4
VMEM_BYTES = 20 * 1024 * 1024
BF16 = jnp.bfloat16
F32 = jnp.float32
HIGHEST = lax.Precision.HIGHEST


def dot(a, b, dims=((1,), (0,)), precision=None):
    return lax.dot_general(a, b, (dims, ((), ())), precision=precision, preferred_element_type=F32)


def picks(routes, gates, base=0):
    tok_count = routes.shape[1]
    shape = (N_XL * SLOT, tok_count)
    row = lax.broadcasted_iota(jnp.int32, shape, 0)
    expert = sum((row >= SLOT * i).astype(jnp.int32) for i in range(1, N_XL))
    slot = (row - SLOT * expert).astype(F32)
    expert = expert + base
    expert = jnp.where(expert >= N_XL, expert - N_XL, expert)
    first = routes[0:1, :] == expert
    second = routes[1:2, :] == expert
    member = jnp.where(first | second, 1.0, 0.0).astype(F32)
    at = lax.broadcasted_iota(jnp.int32, (tok_count, tok_count), 0)
    to = lax.broadcasted_iota(jnp.int32, (tok_count, tok_count), 1)
    earlier = jnp.where(at < to, 1.0, 0.0).astype(BF16)
    rank = dot(member.astype(BF16), earlier)
    pick = jnp.where(rank == slot, member, 0.0)
    gate = jnp.where(first, gates[0:1, :], gates[1:2, :]) * pick
    return pick, gate


def squeeze_matrix(rows, slots):
    row = lax.broadcasted_iota(jnp.int32, (rows, slots), 0)
    col = lax.broadcasted_iota(jnp.int32, (rows, slots), 1)
    expert = sum((row >= CAP * i).astype(jnp.int32) for i in range(1, N_XL))
    return jnp.where(col == row + (SLOT - CAP) * expert, 1.0, 0.0).astype(BF16)


def fetch_rows(pairs, sems):
    cuts = []
    for i, (a, b) in enumerate(pairs):
        step = a.shape[1] // CUTS
        at = [pl.ds(step * k, step) for k in range(CUTS)]
        cuts.append([pltpu.make_async_copy(a.at[:, r], b.at[:, r], sems.at[CUTS * i + k]) for k, r in enumerate(at)])
    for group in cuts:
        for copy in group:
            copy.start()
    return cuts


def fetch(pairs, sems):
    copies = [pltpu.make_async_copy(a, b, sems.at[i]) for i, (a, b) in enumerate(pairs)]
    for copy in copies:
        copy.start()
    return copies


def wait_all(copies):
    for copy in copies:
        copy.wait()


def dispatch(flags, routes_at, gates_at, tokens, cotangent, *refs):
    rows_out, (routes, gates, source, sem, sems) = refs[:N_XL], refs[N_XL:]
    is_x = flags[0] == 0
    copies = fetch(((routes_at, routes), (gates_at, gates)), sems)

    @pl.when(is_x)
    def _():
        pltpu.make_async_copy(tokens, source, sem).start()

    @pl.when(jnp.logical_not(is_x))
    def _():
        pltpu.make_async_copy(cotangent, source, sem).start()

    for copy in copies:
        copy.wait()
    pick, gate = picks(routes[...], gates[...], flags[3])
    scale = jnp.where(is_x, 1.0, jnp.sum(gate, axis=1, keepdims=True))
    pltpu.make_async_copy(tokens, source, sem).wait()
    rows = (dot(pick.astype(BF16), source[...]) * scale).astype(BF16)
    for k in range(N_XL):
        rows_out[k][...] = rows[SLOT * k : SLOT * (k + 1)]


def squeeze(flags, *refs):
    parts, (full_out, cols_out, cols, sems) = refs[:N_XL], refs[N_XL:]
    rows = jnp.concatenate([part[...] for part in parts], axis=0)
    matrix = squeeze_matrix(full_out.shape[0], rows.shape[0])
    full = dot(matrix, rows).astype(BF16)
    full_out[...] = full
    half = full.shape[1] // 2
    part = half // N_Z

    def write(swapped):
        for i in range(N_Z):
            low = full[:, part * i : part * (i + 1)]
            high = full[:, half + part * i : half + part * (i + 1)]
            cols[i] = jnp.concatenate([high, low] if swapped else [low, high], axis=1)

    @pl.when(flags[1] == 0)
    def _():
        write(False)

    @pl.when(flags[1] != 0)
    def _():
        write(True)

    wait_all(fetch([(cols.at[i], cols_out.at[i]) for i in range(N_Z)], sems))


def expert_front(flags, mine, other, gate_w, up_w, down_w, pieces_out, gate_v, up_v, down_v, sems):
    copies = fetch_rows(((gate_w, gate_v), (up_w, up_v), (down_w, down_v)), sems)
    is_x = flags[0] == 0
    a, b = mine[...], other[...]
    x = jnp.where(is_x, a, b)
    dy = jnp.where(is_x, b, a)
    wait_all(copies[0])
    gate_act = dot(x, gate_v[0], ((1,), (1,)))
    wait_all(copies[1])
    up_act = dot(x, up_v[0], ((1,), (1,)))
    wait_all(copies[2])
    hidden_grad = dot(dy, down_v[0], ((1,), (1,)))
    s = 1.0 / (1.0 + jnp.exp(-gate_act))
    silu = gate_act * s
    hidden = (silu * up_act).astype(BF16)
    gate_grad = (hidden_grad * up_act * s * (1.0 + gate_act * (1.0 - s))).astype(BF16)
    up_grad = (hidden_grad * silu).astype(BF16)
    pieces_out[...] = jnp.concatenate([hidden, gate_grad, up_grad], axis=1)


def expert_back(
    flags, pieces, gate_w, up_w, down_w, keep_out, send_out, gate_v, up_v, down_v, sems
):
    copies = fetch_rows(((down_w, down_v), (gate_w, gate_v), (up_w, up_v)), sems)
    ff = pieces.shape[1] // 3
    matrix = squeeze_matrix(pieces.shape[0], N_XL * SLOT)
    held = dot(matrix, pieces[...], ((0,), (0,))).astype(BF16)
    hidden = held[:, :ff]
    gate_grad = held[:, ff : 2 * ff]
    up_grad = held[:, 2 * ff :]
    wait_all(copies[0])
    out = dot(hidden, down_v[0]).astype(BF16)
    wait_all(copies[1])
    wait_all(copies[2])
    back = (dot(gate_grad, gate_v[0]) + dot(up_grad, up_v[0])).astype(BF16)
    part = out.shape[1] // (2 * N_Y)

    def write(even, odd):
        for i in range(N_Y):
            for j, ref in ((2 * i, even), (2 * i + 1, odd)):
                at = slice(part * j, part * (j + 1))
                both = jnp.concatenate([out[:, at], back[:, at]], axis=1)
                for k in range(N_XL):
                    source = lax.rem(flags[3] + (N_XL - k), N_XL)
                    ref[i, source] = both[SLOT * k : SLOT * (k + 1)]

    @pl.when(flags[0] == 0)
    def _():
        write(keep_out, send_out)

    @pl.when(flags[0] != 0)
    def _():
        write(send_out, keep_out)


def combine(routes, gates, blocks, layer_out, grad_out):
    pick, gate = picks(routes[...], gates[...])
    part = layer_out.shape[1]
    experts = []
    for e in range(N_XL):
        total = blocks[e].astype(F32)
        for i in range(1, N_Y):
            total = total + blocks[N_XL * i + e].astype(F32)
        experts.append(total.astype(BF16))
    both = jnp.concatenate(experts, axis=0)
    layer_out[...] = dot(gate, both[:, :part].astype(F32), ((0,), (0,)), HIGHEST).astype(BF16)
    grad_out[...] = dot(pick.astype(BF16), both[:, part:], ((0,), (0,))).astype(BF16)


def grads_of(flags, mine, other, distances, rows):
    is_x = flags[0] == 0
    order = [lax.rem(flags[2] + (N_Z - k), N_Z) for k in distances]
    a = jnp.concatenate([mine[k] for k in order], axis=0)
    b = jnp.concatenate([other[k] for k in order], axis=0)
    x = jnp.where(is_x, a, b)
    dy = jnp.where(is_x, b, a)
    ff = rows.shape[1] // 3
    down = dot(dy, rows[:, :ff], ((0,), (0,)))
    gate_up = dot(x, rows[:, ff:], ((0,), (0,)))
    return jnp.concatenate([down, gate_up], axis=1)


def weight_grads(flags, mine, other, *refs):
    *pieces, total_out, held, sems = refs
    count = pieces[0].shape[0]
    places = [held.at[pl.ds(count * i, count)] for i in range(len(SOON))]
    wait_all(fetch(list(zip(pieces, places)), sems))
    total_out[...] = grads_of(flags, mine, other, SOON, held[...])


def weight_grads_last(flags, mine, other, total, *refs):
    *pieces, keep_out, send_out = refs
    rows = jnp.concatenate([piece[...] for piece in pieces], axis=0)
    both = total[...] + grads_of(flags, mine, other, LAST, rows)
    part = keep_out.shape[0]
    keep_out[...] = both[:part]
    send_out[...] = both[part:].astype(BF16)


def finish(keep, got, gate_out, up_out, down_out):
    total = keep[...] + got[...].astype(F32)
    ff = total.shape[1] // 3
    down_out[0] = total[:, :ff]
    gate_out[0] = total[:, ff : 2 * ff]
    up_out[0] = total[:, 2 * ff :]


def call(body, outs, scalars, *operands, far=(), scratch=(), flops=0, far_outs=0):
    vmem = pl.BlockSpec(memory_space=pltpu.VMEM)
    smem = pl.BlockSpec(memory_space=pltpu.SMEM)
    hbm = pl.BlockSpec(memory_space=pltpu.HBM)
    moved = sum(v.size * v.dtype.itemsize for v in (*operands, *far))
    cost = pl.CostEstimate(flops=flops, transcendentals=0, bytes_accessed=moved)
    return pl.pallas_call(
        body,
        out_shape=[
            jax.ShapeDtypeStruct(s, t) if i < len(outs) - far_outs else pltpu.HBM(s, t)
            for i, (s, t) in enumerate(outs)
        ],
        in_specs=[smem] * len(scalars)
        + [vmem] * len(operands)
        + [hbm] * len(far),
        out_specs=[vmem] * (len(outs) - far_outs) + [hbm] * far_outs,
        scratch_shapes=list(scratch),
        compiler_params=pltpu.CompilerParams(vmem_limit_bytes=VMEM_BYTES),
        cost_estimate=cost if flops else None,
        name=body.__name__,
    )(*scalars, *operands, *[pltpu.with_memory_space_constraint(v, pltpu.HBM) for v in far])


def shift(value, by):
    return lax.ppermute(value, "z", [(i, (i + by) % N_Z) for i in range(N_Z)])


def spread(parts, axis, forward=1):
    count = len(parts)
    return [parts[0]] + [
        lax.ppermute(parts[k], axis, [(i, (i + forward * k) % count) for i in range(count)])
        for k in range(1, count)
    ]


def swap(value, axis):
    return lax.ppermute(value, axis, [(0, 1), (1, 0)])


def on_device(tokens, cotangent, routes, router_gates, gate_weight, up_weight, down_weight):
    width = tokens.shape[1]
    tok_count = tokens.shape[0]
    ff = gate_weight.shape[2]
    part = width // 16
    slots = N_XL * SLOT
    rows = N_XL * CAP
    work = 3 * 2 * rows * width * ff
    flags = jnp.stack([lax.axis_index(a) for a in ("c", "xh", "z", "xl", "y")]).astype(jnp.int32)
    routes = routes.T
    gates = router_gates.T
    weights = (jnp.swapaxes(gate_weight, 1, 2), jnp.swapaxes(up_weight, 1, 2), down_weight)
    held = [pltpu.VMEM(w.shape, BF16) for w in weights]
    held.append(pltpu.SemaphoreType.DMA((3 * CUTS,)))

    sent = call(
        dispatch,
        [((SLOT, width), BF16)] * N_XL,
        [flags],
        far=(routes, gates, tokens, cotangent),
        scratch=(
            pltpu.VMEM(routes.shape, routes.dtype),
            pltpu.VMEM(gates.shape, gates.dtype),
            pltpu.VMEM(tokens.shape, BF16),
            pltpu.SemaphoreType.DMA,
            pltpu.SemaphoreType.DMA((2,)),
        ),
    )
    got = spread(sent, "xl")
    mine, cols = call(
        squeeze,
        [((rows, width), BF16), ((N_Z, rows, 2 * part), BF16)],
        [flags],
        *got,
        scratch=(pltpu.VMEM((N_Z, rows, 2 * part), BF16), pltpu.SemaphoreType.DMA((N_Z,))),
        far_outs=1,
    )
    other = swap(mine, "c")
    cols = lax.all_to_all(cols, "z", split_axis=0, concat_axis=0, tiled=True)
    (pieces,) = call(
        expert_front, [((rows, 3 * ff), BF16)], [flags], mine, other, far=weights, scratch=held
    )
    keep, send = call(
        expert_back,
        [((N_Y, N_XL, SLOT, 2 * part), BF16)] * 2,
        [flags],
        pieces,
        far=weights,
        scratch=held,
        flops=work,
    )
    summed = (keep.astype(F32) + swap(send, "c").astype(F32)).astype(BF16)

    found = [pieces] + [None] * (N_Z - 1)
    for k in range(1, N_Z // 2):
        found[k] = shift(found[k - 1], 1)
        found[N_Z - k] = shift(found[(N_Z - k + 1) % N_Z], -1)
    found[N_Z // 2] = shift(found[N_Z // 2 - 1], 1)
    cols_other = swap(cols, "c")

    summed, _ = lax.optimization_barrier((summed, (found[1], found[7])))
    blocks = lax.all_to_all(
        summed.reshape(N_Y * N_XL, SLOT, 2 * part),
        ("y", "xl"),
        split_axis=0,
        concat_axis=0,
        tiled=True,
    )
    layer_out, token_grad = call(
        combine, [((tok_count, part), BF16)] * 2, [], routes, gates, blocks
    )

    (total,) = call(
        weight_grads,
        [((2 * part, 3 * ff), F32)],
        [flags],
        cols,
        cols_other,
        far=[found[k] for k in SOON],
        scratch=(
            pltpu.VMEM((len(SOON) * rows, 3 * ff), BF16),
            pltpu.SemaphoreType.DMA((len(SOON),)),
        ),
        flops=2 * len(SOON) * rows * 2 * part * 3 * ff,
    )
    kept, given = call(
        weight_grads_last,
        [((part, 3 * ff), F32), ((part, 3 * ff), BF16)],
        [flags],
        cols,
        cols_other,
        total,
        *[found[k] for k in LAST],
    )
    grad_gate, grad_up, grad_down = call(
        finish, [((1, part, ff), F32)] * 3, [], kept, swap(given, "xh")
    )
    return layer_out, token_grad, grad_gate, grad_up, jnp.swapaxes(grad_down, 1, 2)


def solution(mesh):
    fine = Mesh(
        mesh.devices.reshape(2, N_Z, N_XL, N_Y, 2), ("xh", "z", "xl", "y", "c")
    )
    seq, ffn = ("xh", "z"), ("y", "c")
    rows = P(("xh", "z", "xl"), None)
    return jax.shard_map(
        on_device,
        mesh=fine,
        in_specs=(
            rows,
            rows,
            rows,
            rows,
            P("xl", None, ffn),
            P("xl", None, ffn),
            P("xl", ffn, None),
        ),
        out_specs=(
            P(("xh", "z", "xl"), ffn),
            P(("xh", "z", "xl"), ffn),
            P("xl", seq, ffn),
            P("xl", seq, ffn),
            P("xl", ffn, seq),
        ),
        check_vma=False,
    )
```

```python
import jax
import jax.numpy as jnp
from jax import lax
from jax.experimental import pallas as pl
from jax.experimental.pallas import tpu as pltpu
from jax.sharding import Mesh, PartitionSpec as P

CAP = 36
SLOT = 40
SOON = (0, 1, 7, 2, 6, 3)
LAST = (5, 4)
CUTS = 3
N_Z = 8
N_Y = 8
N_XL = 4
VMEM_BYTES = 20 * 1024 * 1024
BF16 = jnp.bfloat16
F32 = jnp.float32
HIGHEST = lax.Precision.HIGHEST


def dot(a, b, dims=((1,), (0,)), precision=None):
    return lax.dot_general(a, b, (dims, ((), ())), precision=precision, preferred_element_type=F32)


def picks(routes, gates, base=0):
    tok_count = routes.shape[1]
    shape = (N_XL * SLOT, tok_count)
    row = lax.broadcasted_iota(jnp.int32, shape, 0)
    expert = sum((row >= SLOT * i).astype(jnp.int32) for i in range(1, N_XL))
    slot = (row - SLOT * expert).astype(F32)
    expert = expert + base
    expert = jnp.where(expert >= N_XL, expert - N_XL, expert)
    first = routes[0:1, :] == expert
    second = routes[1:2, :] == expert
    member = jnp.where(first | second, 1.0, 0.0).astype(F32)
    at = lax.broadcasted_iota(jnp.int32, (tok_count, tok_count), 0)
    to = lax.broadcasted_iota(jnp.int32, (tok_count, tok_count), 1)
    earlier = jnp.where(at < to, 1.0, 0.0).astype(BF16)
    rank = dot(member.astype(BF16), earlier)
    pick = jnp.where(rank == slot, member, 0.0)
    gate = jnp.where(first, gates[0:1, :], gates[1:2, :]) * pick
    return pick, gate


def squeeze_matrix(rows, slots):
    row = lax.broadcasted_iota(jnp.int32, (rows, slots), 0)
    col = lax.broadcasted_iota(jnp.int32, (rows, slots), 1)
    expert = sum((row >= CAP * i).astype(jnp.int32) for i in range(1, N_XL))
    return jnp.where(col == row + (SLOT - CAP) * expert, 1.0, 0.0).astype(BF16)


def fetch_rows(pairs, sems):
    cuts = []
    for i, (a, b) in enumerate(pairs):
        step = a.shape[1] // CUTS
        at = [pl.ds(step * k, step) for k in range(CUTS)]
        cuts.append([pltpu.make_async_copy(a.at[:, r], b.at[:, r], sems.at[CUTS * i + k]) for k, r in enumerate(at)])
    for group in cuts:
        for copy in group:
            copy.start()
    return cuts


def fetch(pairs, sems):
    copies = [pltpu.make_async_copy(a, b, sems.at[i]) for i, (a, b) in enumerate(pairs)]
    for copy in copies:
        copy.start()
    return copies


def wait_all(copies):
    for copy in copies:
        copy.wait()


def dispatch(flags, routes_at, gates_at, tokens, cotangent, *refs):
    rows_out, (routes, gates, source, sem, sems) = refs[:N_XL], refs[N_XL:]
    is_x = flags[0] == 0
    copies = fetch(((routes_at, routes), (gates_at, gates)), sems)

    @pl.when(is_x)
    def _():
        pltpu.make_async_copy(tokens, source, sem).start()

    @pl.when(jnp.logical_not(is_x))
    def _():
        pltpu.make_async_copy(cotangent, source, sem).start()

    for copy in copies:
        copy.wait()
    pick, gate = picks(routes[...], gates[...], flags[3])
    scale = jnp.where(is_x, 1.0, jnp.sum(gate, axis=1, keepdims=True))
    pltpu.make_async_copy(tokens, source, sem).wait()
    rows = (dot(pick.astype(BF16), source[...]) * scale).astype(BF16)
    for k in range(N_XL):
        rows_out[k][...] = rows[SLOT * k : SLOT * (k + 1)]


def squeeze(flags, *refs):
    parts, (full_out, cols_out, cols, sems) = refs[:N_XL], refs[N_XL:]
    rows = jnp.concatenate([part[...] for part in parts], axis=0)
    matrix = squeeze_matrix(full_out.shape[0], rows.shape[0])
    full = dot(matrix, rows).astype(BF16)
    full_out[...] = full
    half = full.shape[1] // 2
    part = half // N_Z

    def write(swapped):
        for i in range(N_Z):
            low = full[:, part * i : part * (i + 1)]
            high = full[:, half + part * i : half + part * (i + 1)]
            cols[i] = jnp.concatenate([high, low] if swapped else [low, high], axis=1)

    @pl.when(flags[1] == 0)
    def _():
        write(False)

    @pl.when(flags[1] != 0)
    def _():
        write(True)

    wait_all(fetch([(cols.at[i], cols_out.at[i]) for i in range(N_Z)], sems))


def expert_front(flags, mine, other, gate_w, up_w, down_w, pieces_out, gate_v, up_v, down_v, sems):
    copies = fetch_rows(((gate_w, gate_v), (up_w, up_v), (down_w, down_v)), sems)
    is_x = flags[0] == 0
    a, b = mine[...], other[...]
    x = jnp.where(is_x, a, b)
    dy = jnp.where(is_x, b, a)
    wait_all(copies[0])
    gate_act = dot(x, gate_v[0], ((1,), (1,)))
    wait_all(copies[1])
    up_act = dot(x, up_v[0], ((1,), (1,)))
    wait_all(copies[2])
    hidden_grad = dot(dy, down_v[0], ((1,), (1,)))
    s = 1.0 / (1.0 + jnp.exp(-gate_act))
    silu = gate_act * s
    hidden = (silu * up_act).astype(BF16)
    gate_grad = (hidden_grad * up_act * s * (1.0 + gate_act * (1.0 - s))).astype(BF16)
    up_grad = (hidden_grad * silu).astype(BF16)
    pieces_out[...] = jnp.concatenate([hidden, gate_grad, up_grad], axis=1)


def expert_back(
    flags, pieces, gate_w, up_w, down_w, keep_out, send_out, gate_v, up_v, down_v, sems
):
    copies = fetch_rows(((down_w, down_v), (gate_w, gate_v), (up_w, up_v)), sems)
    ff = pieces.shape[1] // 3
    matrix = squeeze_matrix(pieces.shape[0], N_XL * SLOT)
    held = dot(matrix, pieces[...], ((0,), (0,))).astype(BF16)
    hidden = held[:, :ff]
    gate_grad = held[:, ff : 2 * ff]
    up_grad = held[:, 2 * ff :]
    wait_all(copies[0])
    out = dot(hidden, down_v[0]).astype(BF16)
    wait_all(copies[1])
    wait_all(copies[2])
    back = (dot(gate_grad, gate_v[0]) + dot(up_grad, up_v[0])).astype(BF16)
    part = out.shape[1] // (2 * N_Y)

    def write(even, odd):
        for i in range(N_Y):
            for j, ref in ((2 * i, even), (2 * i + 1, odd)):
                at = slice(part * j, part * (j + 1))
                both = jnp.concatenate([out[:, at], back[:, at]], axis=1)
                for k in range(N_XL):
                    source = lax.rem(flags[3] + (N_XL - k), N_XL)
                    ref[source, i] = both[SLOT * k : SLOT * (k + 1)]

    @pl.when(flags[0] == 0)
    def _():
        write(keep_out, send_out)

    @pl.when(flags[0] != 0)
    def _():
        write(send_out, keep_out)


def combine(routes, gates, blocks, layer_out, grad_out):
    pick, gate = picks(routes[...], gates[...])
    part = layer_out.shape[1]
    experts = []
    for e in range(N_XL):
        total = blocks[N_Y * e].astype(F32)
        for i in range(1, N_Y):
            total = total + blocks[N_Y * e + i].astype(F32)
        experts.append(total.astype(BF16))
    both = jnp.concatenate(experts, axis=0)
    layer_out[...] = dot(gate, both[:, :part].astype(F32), ((0,), (0,)), HIGHEST).astype(BF16)
    grad_out[...] = dot(pick.astype(BF16), both[:, part:], ((0,), (0,))).astype(BF16)


def grads_of(flags, mine, other, distances, rows):
    is_x = flags[0] == 0
    order = [lax.rem(flags[2] + (N_Z - k), N_Z) for k in distances]
    a = jnp.concatenate([mine[k] for k in order], axis=0)
    b = jnp.concatenate([other[k] for k in order], axis=0)
    x = jnp.where(is_x, a, b)
    dy = jnp.where(is_x, b, a)
    ff = rows.shape[1] // 3
    down = dot(dy, rows[:, :ff], ((0,), (0,)))
    gate_up = dot(x, rows[:, ff:], ((0,), (0,)))
    return jnp.concatenate([down, gate_up], axis=1)


def weight_grads(flags, mine, other, *refs):
    *pieces, total_out, held, sems = refs
    count = pieces[0].shape[0]
    places = [held.at[pl.ds(count * i, count)] for i in range(len(SOON))]
    wait_all(fetch(list(zip(pieces, places)), sems))
    total_out[...] = grads_of(flags, mine, other, SOON, held[...])


def weight_grads_last(flags, mine, other, total, *refs):
    *pieces, keep_out, send_out = refs
    rows = jnp.concatenate([piece[...] for piece in pieces], axis=0)
    both = total[...] + grads_of(flags, mine, other, LAST, rows)
    part = keep_out.shape[0]
    keep_out[...] = both[:part]
    send_out[...] = both[part:].astype(BF16)


def finish(keep, got, gate_out, up_out, down_out):
    total = keep[...] + got[...].astype(F32)
    ff = total.shape[1] // 3
    down_out[0] = total[:, :ff]
    gate_out[0] = total[:, ff : 2 * ff]
    up_out[0] = total[:, 2 * ff :]


def call(body, outs, scalars, *operands, far=(), scratch=(), flops=0, far_outs=0):
    vmem = pl.BlockSpec(memory_space=pltpu.VMEM)
    smem = pl.BlockSpec(memory_space=pltpu.SMEM)
    hbm = pl.BlockSpec(memory_space=pltpu.HBM)
    moved = sum(v.size * v.dtype.itemsize for v in (*operands, *far))
    cost = pl.CostEstimate(flops=flops, transcendentals=0, bytes_accessed=moved)
    return pl.pallas_call(
        body,
        out_shape=[
            jax.ShapeDtypeStruct(s, t) if i < len(outs) - far_outs else pltpu.HBM(s, t)
            for i, (s, t) in enumerate(outs)
        ],
        in_specs=[smem] * len(scalars)
        + [vmem] * len(operands)
        + [hbm] * len(far),
        out_specs=[vmem] * (len(outs) - far_outs) + [hbm] * far_outs,
        scratch_shapes=list(scratch),
        compiler_params=pltpu.CompilerParams(vmem_limit_bytes=VMEM_BYTES),
        cost_estimate=cost if flops else None,
        name=body.__name__,
    )(*scalars, *operands, *[pltpu.with_memory_space_constraint(v, pltpu.HBM) for v in far])


def shift(value, by):
    return lax.ppermute(value, "z", [(i, (i + by) % N_Z) for i in range(N_Z)])


def spread(parts, axis, forward=1):
    count = len(parts)
    return [parts[0]] + [
        lax.ppermute(parts[k], axis, [(i, (i + forward * k) % count) for i in range(count)])
        for k in range(1, count)
    ]


def swap(value, axis):
    return lax.ppermute(value, axis, [(0, 1), (1, 0)])


def on_device(tokens, cotangent, routes, router_gates, gate_weight, up_weight, down_weight):
    width = tokens.shape[1]
    tok_count = tokens.shape[0]
    ff = gate_weight.shape[2]
    part = width // 16
    slots = N_XL * SLOT
    rows = N_XL * CAP
    work = 3 * 2 * rows * width * ff
    flags = jnp.stack([lax.axis_index(a) for a in ("c", "xh", "z", "xl", "y")]).astype(jnp.int32)
    routes = routes.T
    gates = router_gates.T
    weights = (jnp.swapaxes(gate_weight, 1, 2), jnp.swapaxes(up_weight, 1, 2), down_weight)
    held = [pltpu.VMEM(w.shape, BF16) for w in weights]
    held.append(pltpu.SemaphoreType.DMA((3 * CUTS,)))

    sent = call(
        dispatch,
        [((SLOT, width), BF16)] * N_XL,
        [flags],
        far=(routes, gates, tokens, cotangent),
        scratch=(
            pltpu.VMEM(routes.shape, routes.dtype),
            pltpu.VMEM(gates.shape, gates.dtype),
            pltpu.VMEM(tokens.shape, BF16),
            pltpu.SemaphoreType.DMA,
            pltpu.SemaphoreType.DMA((2,)),
        ),
    )
    got = spread(sent, "xl")
    mine, cols = call(
        squeeze,
        [((rows, width), BF16), ((N_Z, rows, 2 * part), BF16)],
        [flags],
        *got,
        scratch=(pltpu.VMEM((N_Z, rows, 2 * part), BF16), pltpu.SemaphoreType.DMA((N_Z,))),
        far_outs=1,
    )
    other = swap(mine, "c")
    cols = lax.all_to_all(cols, "z", split_axis=0, concat_axis=0, tiled=True)
    (pieces,) = call(
        expert_front, [((rows, 3 * ff), BF16)], [flags], mine, other, far=weights, scratch=held
    )
    keep, send = call(
        expert_back,
        [((N_XL, N_Y, SLOT, 2 * part), BF16)] * 2,
        [flags],
        pieces,
        far=weights,
        scratch=held,
        flops=work,
    )
    summed = (keep.astype(F32) + swap(send, "c").astype(F32)).astype(BF16)

    found = [pieces] + [None] * (N_Z - 1)
    for k in range(1, N_Z // 2):
        found[k] = shift(found[k - 1], 1)
        found[N_Z - k] = shift(found[(N_Z - k + 1) % N_Z], -1)
    found[N_Z // 2] = shift(found[N_Z // 2 - 1], 1)
    cols_other = swap(cols, "c")

    summed, _ = lax.optimization_barrier((summed, (found[1], found[7])))
    blocks = lax.all_to_all(
        summed.reshape(N_XL * N_Y, SLOT, 2 * part),
        ("xl", "y"),
        split_axis=0,
        concat_axis=0,
        tiled=True,
    )
    layer_out, token_grad = call(
        combine, [((tok_count, part), BF16)] * 2, [], routes, gates, blocks
    )

    (total,) = call(
        weight_grads,
        [((2 * part, 3 * ff), F32)],
        [flags],
        cols,
        cols_other,
        far=[found[k] for k in SOON],
        scratch=(
            pltpu.VMEM((len(SOON) * rows, 3 * ff), BF16),
            pltpu.SemaphoreType.DMA((len(SOON),)),
        ),
        flops=2 * len(SOON) * rows * 2 * part * 3 * ff,
    )
    kept, given = call(
        weight_grads_last,
        [((part, 3 * ff), F32), ((part, 3 * ff), BF16)],
        [flags],
        cols,
        cols_other,
        total,
        *[found[k] for k in LAST],
    )
    received, layer_out, token_grad = lax.optimization_barrier(
        (swap(given, "xh"), layer_out, token_grad)
    )
    grad_gate, grad_up, grad_down = call(
        finish, [((1, part, ff), F32)] * 3, [], kept, received
    )
    return layer_out, token_grad, grad_gate, grad_up, jnp.swapaxes(grad_down, 1, 2)


def solution(mesh):
    fine = Mesh(
        mesh.devices.reshape(2, N_Z, N_XL, N_Y, 2), ("xh", "z", "xl", "y", "c")
    )
    seq, ffn = ("xh", "z"), ("y", "c")
    rows = P(("xh", "z", "xl"), None)
    return jax.shard_map(
        on_device,
        mesh=fine,
        in_specs=(
            rows,
            rows,
            rows,
            rows,
            P("xl", None, ffn),
            P("xl", None, ffn),
            P("xl", ffn, None),
        ),
        out_specs=(
            P(("xh", "z", "xl"), ffn),
            P(("xh", "z", "xl"), ffn),
            P("xl", seq, ffn),
            P("xl", seq, ffn),
            P("xl", ffn, seq),
        ),
        check_vma=False,
    )
```

```python
import jax
import jax.numpy as jnp
from jax import lax
from jax.experimental import pallas as pl
from jax.experimental.pallas import tpu as pltpu
from jax.sharding import Mesh, PartitionSpec as P

CAP = 36
SLOT = 40
SOON = (0, 1, 7, 2, 6, 3)
LAST = (5, 4)
CUTS = 3
N_Z = 8
N_Y = 8
N_XL = 4
VMEM_BYTES = 20 * 1024 * 1024
BF16 = jnp.bfloat16
F32 = jnp.float32
HIGHEST = lax.Precision.HIGHEST


def dot(a, b, dims=((1,), (0,)), precision=None):
    return lax.dot_general(a, b, (dims, ((), ())), precision=precision, preferred_element_type=F32)


def picks(routes, gates, base=0):
    tok_count = routes.shape[1]
    shape = (N_XL * SLOT, tok_count)
    row = lax.broadcasted_iota(jnp.int32, shape, 0)
    expert = sum((row >= SLOT * i).astype(jnp.int32) for i in range(1, N_XL))
    slot = (row - SLOT * expert).astype(F32)
    expert = expert + base
    expert = jnp.where(expert >= N_XL, expert - N_XL, expert)
    first = routes[0:1, :] == expert
    second = routes[1:2, :] == expert
    member = jnp.where(first | second, 1.0, 0.0).astype(F32)
    at = lax.broadcasted_iota(jnp.int32, (tok_count, tok_count), 0)
    to = lax.broadcasted_iota(jnp.int32, (tok_count, tok_count), 1)
    earlier = jnp.where(at < to, 1.0, 0.0).astype(BF16)
    rank = dot(member.astype(BF16), earlier)
    pick = jnp.where(rank == slot, member, 0.0)
    gate = jnp.where(first, gates[0:1, :], gates[1:2, :]) * pick
    return pick, gate


def squeeze_matrix(rows, slots):
    row = lax.broadcasted_iota(jnp.int32, (rows, slots), 0)
    col = lax.broadcasted_iota(jnp.int32, (rows, slots), 1)
    expert = sum((row >= CAP * i).astype(jnp.int32) for i in range(1, N_XL))
    return jnp.where(col == row + (SLOT - CAP) * expert, 1.0, 0.0).astype(BF16)


def fetch_rows(pairs, sems):
    cuts = []
    for i, (a, b) in enumerate(pairs):
        step = a.shape[1] // CUTS
        at = [pl.ds(step * k, step) for k in range(CUTS)]
        cuts.append([pltpu.make_async_copy(a.at[:, r], b.at[:, r], sems.at[CUTS * i + k]) for k, r in enumerate(at)])
    for group in cuts:
        for copy in group:
            copy.start()
    return cuts


def fetch(pairs, sems):
    copies = [pltpu.make_async_copy(a, b, sems.at[i]) for i, (a, b) in enumerate(pairs)]
    for copy in copies:
        copy.start()
    return copies


def wait_all(copies):
    for copy in copies:
        copy.wait()


def dispatch(flags, routes_at, gates_at, tokens, cotangent, *refs):
    rows_out, (routes, gates, source, sem, sems) = refs[:N_XL], refs[N_XL:]
    is_x = flags[0] == 0
    copies = fetch(((routes_at, routes), (gates_at, gates)), sems)

    @pl.when(is_x)
    def _():
        pltpu.make_async_copy(tokens, source, sem).start()

    @pl.when(jnp.logical_not(is_x))
    def _():
        pltpu.make_async_copy(cotangent, source, sem).start()

    for copy in copies:
        copy.wait()
    pick, gate = picks(routes[...], gates[...], flags[3])
    scale = jnp.where(is_x, 1.0, jnp.sum(gate, axis=1, keepdims=True))
    pltpu.make_async_copy(tokens, source, sem).wait()
    rows = (dot(pick.astype(BF16), source[...]) * scale).astype(BF16)
    for k in range(N_XL):
        rows_out[k][...] = rows[SLOT * k : SLOT * (k + 1)]


def squeeze(flags, *refs):
    parts, (full_out, cols_out, cols, sems) = refs[:N_XL], refs[N_XL:]
    rows = jnp.concatenate([part[...] for part in parts], axis=0)
    matrix = squeeze_matrix(full_out.shape[0], rows.shape[0])
    full = dot(matrix, rows).astype(BF16)
    full_out[...] = full
    half = full.shape[1] // 2
    part = half // N_Z

    def write(swapped):
        for i in range(N_Z):
            low = full[:, part * i : part * (i + 1)]
            high = full[:, half + part * i : half + part * (i + 1)]
            cols[i] = jnp.concatenate([high, low] if swapped else [low, high], axis=1)

    @pl.when(flags[1] == 0)
    def _():
        write(False)

    @pl.when(flags[1] != 0)
    def _():
        write(True)

    wait_all(fetch([(cols.at[i], cols_out.at[i]) for i in range(N_Z)], sems))


def expert_front(flags, mine, other, gate_w, up_w, down_w, pieces_out, gate_v, up_v, down_v, sems):
    copies = fetch_rows(((gate_w, gate_v), (up_w, up_v), (down_w, down_v)), sems)
    is_x = flags[0] == 0
    a, b = mine[...], other[...]
    x = jnp.where(is_x, a, b)
    dy = jnp.where(is_x, b, a)
    wait_all(copies[0])
    gate_act = dot(x, gate_v[0], ((1,), (1,)))
    wait_all(copies[1])
    up_act = dot(x, up_v[0], ((1,), (1,)))
    wait_all(copies[2])
    hidden_grad = dot(dy, down_v[0], ((1,), (1,)))
    s = 1.0 / (1.0 + jnp.exp(-gate_act))
    silu = gate_act * s
    hidden = (silu * up_act).astype(BF16)
    gate_grad = (hidden_grad * up_act * s * (1.0 + gate_act * (1.0 - s))).astype(BF16)
    up_grad = (hidden_grad * silu).astype(BF16)
    pieces_out[...] = jnp.concatenate([hidden, gate_grad, up_grad], axis=1)


def expert_back(
    flags, pieces, gate_w, up_w, down_w, keep_out, send_out, gate_v, up_v, down_v, sems
):
    copies = fetch_rows(((down_w, down_v), (gate_w, gate_v), (up_w, up_v)), sems)
    ff = pieces.shape[1] // 3
    hidden = pieces[:, :ff]
    gate_grad = pieces[:, ff : 2 * ff]
    up_grad = pieces[:, 2 * ff :]
    wait_all(copies[0])
    out = dot(hidden, down_v[0]).astype(BF16)
    wait_all(copies[1])
    wait_all(copies[2])
    back = (dot(gate_grad, gate_v[0]) + dot(up_grad, up_v[0])).astype(BF16)
    part = out.shape[1] // (2 * N_Y)

    def write(even, odd):
        for i in range(N_Y):
            for j, ref in ((2 * i, even), (2 * i + 1, odd)):
                at = slice(part * j, part * (j + 1))
                ref[i] = jnp.concatenate([out[:, at], back[:, at]], axis=1)

    @pl.when(flags[0] == 0)
    def _():
        write(keep_out, send_out)

    @pl.when(flags[0] != 0)
    def _():
        write(send_out, keep_out)


def add_up(flags, blocks, rows_out):
    total = blocks[0].astype(F32)
    for i in range(1, N_Y):
        total = total + blocks[i].astype(F32)
    spread_out = squeeze_matrix(total.shape[0], N_XL * SLOT)
    rows = dot(spread_out, total.astype(BF16), ((0,), (0,))).astype(BF16)
    for k in range(N_XL):
        rows_out[lax.rem(flags[3] + (N_XL - k), N_XL)] = rows[SLOT * k : SLOT * (k + 1)]


def combine(routes, gates, rows, layer_out, grad_out):
    pick, gate = picks(routes[...], gates[...])
    part = layer_out.shape[1]
    both = rows[...]
    layer_out[...] = dot(gate, both[:, :part].astype(F32), ((0,), (0,)), HIGHEST).astype(BF16)
    grad_out[...] = dot(pick.astype(BF16), both[:, part:], ((0,), (0,))).astype(BF16)


def grads_of(flags, mine, other, distances, rows):
    is_x = flags[0] == 0
    order = [lax.rem(flags[2] + (N_Z - k), N_Z) for k in distances]
    a = jnp.concatenate([mine[k] for k in order], axis=0)
    b = jnp.concatenate([other[k] for k in order], axis=0)
    x = jnp.where(is_x, a, b)
    dy = jnp.where(is_x, b, a)
    ff = rows.shape[1] // 3
    down = dot(dy, rows[:, :ff], ((0,), (0,)))
    gate_up = dot(x, rows[:, ff:], ((0,), (0,)))
    return jnp.concatenate([down, gate_up], axis=1)


def weight_grads(flags, mine, other, *refs):
    *pieces, total_out, held, sems = refs
    count = pieces[0].shape[0]
    places = [held.at[pl.ds(count * i, count)] for i in range(len(SOON))]
    wait_all(fetch(list(zip(pieces, places)), sems))
    total_out[...] = grads_of(flags, mine, other, SOON, held[...])


def weight_grads_last(flags, mine, other, total, *refs):
    *pieces, keep_out, send_out = refs
    rows = jnp.concatenate([piece[...] for piece in pieces], axis=0)
    both = total[...] + grads_of(flags, mine, other, LAST, rows)
    part = keep_out.shape[0]
    keep_out[...] = both[:part]
    send_out[...] = both[part:].astype(BF16)


def finish(keep, got, gate_out, up_out, down_out):
    total = keep[...] + got[...].astype(F32)
    ff = total.shape[1] // 3
    down_out[0] = total[:, :ff]
    gate_out[0] = total[:, ff : 2 * ff]
    up_out[0] = total[:, 2 * ff :]


def call(body, outs, scalars, *operands, far=(), scratch=(), flops=0, far_outs=0):
    vmem = pl.BlockSpec(memory_space=pltpu.VMEM)
    smem = pl.BlockSpec(memory_space=pltpu.SMEM)
    hbm = pl.BlockSpec(memory_space=pltpu.HBM)
    moved = sum(v.size * v.dtype.itemsize for v in (*operands, *far))
    cost = pl.CostEstimate(flops=flops, transcendentals=0, bytes_accessed=moved)
    return pl.pallas_call(
        body,
        out_shape=[
            jax.ShapeDtypeStruct(s, t) if i < len(outs) - far_outs else pltpu.HBM(s, t)
            for i, (s, t) in enumerate(outs)
        ],
        in_specs=[smem] * len(scalars)
        + [vmem] * len(operands)
        + [hbm] * len(far),
        out_specs=[vmem] * (len(outs) - far_outs) + [hbm] * far_outs,
        scratch_shapes=list(scratch),
        compiler_params=pltpu.CompilerParams(vmem_limit_bytes=VMEM_BYTES),
        cost_estimate=cost if flops else None,
        name=body.__name__,
    )(*scalars, *operands, *[pltpu.with_memory_space_constraint(v, pltpu.HBM) for v in far])


def shift(value, by):
    return lax.ppermute(value, "z", [(i, (i + by) % N_Z) for i in range(N_Z)])


def spread(parts, axis, forward=1):
    count = len(parts)
    return [parts[0]] + [
        lax.ppermute(parts[k], axis, [(i, (i + forward * k) % count) for i in range(count)])
        for k in range(1, count)
    ]


def swap(value, axis):
    return lax.ppermute(value, axis, [(0, 1), (1, 0)])


def on_device(tokens, cotangent, routes, router_gates, gate_weight, up_weight, down_weight):
    width = tokens.shape[1]
    tok_count = tokens.shape[0]
    ff = gate_weight.shape[2]
    part = width // 16
    slots = N_XL * SLOT
    rows = N_XL * CAP
    work = 3 * 2 * rows * width * ff
    flags = jnp.stack([lax.axis_index(a) for a in ("c", "xh", "z", "xl", "y")]).astype(jnp.int32)
    routes = routes.T
    gates = router_gates.T
    weights = (jnp.swapaxes(gate_weight, 1, 2), jnp.swapaxes(up_weight, 1, 2), down_weight)
    held = [pltpu.VMEM(w.shape, BF16) for w in weights]
    held.append(pltpu.SemaphoreType.DMA((3 * CUTS,)))

    sent = call(
        dispatch,
        [((SLOT, width), BF16)] * N_XL,
        [flags],
        far=(routes, gates, tokens, cotangent),
        scratch=(
            pltpu.VMEM(routes.shape, routes.dtype),
            pltpu.VMEM(gates.shape, gates.dtype),
            pltpu.VMEM(tokens.shape, BF16),
            pltpu.SemaphoreType.DMA,
            pltpu.SemaphoreType.DMA((2,)),
        ),
    )
    got = spread(sent, "xl")
    mine, cols = call(
        squeeze,
        [((rows, width), BF16), ((N_Z, rows, 2 * part), BF16)],
        [flags],
        *got,
        scratch=(pltpu.VMEM((N_Z, rows, 2 * part), BF16), pltpu.SemaphoreType.DMA((N_Z,))),
        far_outs=1,
    )
    other = swap(mine, "c")
    cols = lax.all_to_all(cols, "z", split_axis=0, concat_axis=0, tiled=True)
    (pieces,) = call(
        expert_front, [((rows, 3 * ff), BF16)], [flags], mine, other, far=weights, scratch=held
    )
    keep, send = call(
        expert_back,
        [((N_Y, rows, 2 * part), BF16)] * 2,
        [flags],
        pieces,
        far=weights,
        scratch=held,
        flops=work,
    )
    summed = (keep.astype(F32) + swap(send, "c").astype(F32)).astype(BF16)

    found = [pieces] + [None] * (N_Z - 1)
    for k in range(1, N_Z // 2):
        found[k] = shift(found[k - 1], 1)
        found[N_Z - k] = shift(found[(N_Z - k + 1) % N_Z], -1)
    cols_other = swap(cols, "c")

    summed, _ = lax.optimization_barrier((summed, (found[1], found[7])))
    blocks = lax.all_to_all(summed, "y", split_axis=0, concat_axis=0, tiled=True)
    (back,) = call(add_up, [((N_XL, SLOT, 2 * part), BF16)], [flags], blocks)
    found[3], _ = lax.optimization_barrier((found[3], back))
    found[4] = shift(found[3], 1)
    back = lax.all_to_all(back, "xl", split_axis=0, concat_axis=0, tiled=True)
    layer_out, token_grad = call(
        combine,
        [((tok_count, part), BF16)] * 2,
        [],
        routes,
        gates,
        back.reshape(slots, 2 * part),
    )

    (total,) = call(
        weight_grads,
        [((2 * part, 3 * ff), F32)],
        [flags],
        cols,
        cols_other,
        far=[found[k] for k in SOON],
        scratch=(
            pltpu.VMEM((len(SOON) * rows, 3 * ff), BF16),
            pltpu.SemaphoreType.DMA((len(SOON),)),
        ),
        flops=2 * len(SOON) * rows * 2 * part * 3 * ff,
    )
    total, _ = lax.optimization_barrier((total, back))
    kept, given = call(
        weight_grads_last,
        [((part, 3 * ff), F32), ((part, 3 * ff), BF16)],
        [flags],
        cols,
        cols_other,
        total,
        *[found[k] for k in LAST],
    )
    received, layer_out, token_grad = lax.optimization_barrier(
        (swap(given, "xh"), layer_out, token_grad)
    )
    grad_gate, grad_up, grad_down = call(
        finish, [((1, part, ff), F32)] * 3, [], kept, received
    )
    return layer_out, token_grad, grad_gate, grad_up, jnp.swapaxes(grad_down, 1, 2)


def solution(mesh):
    fine = Mesh(
        mesh.devices.reshape(2, N_Z, N_XL, N_Y, 2), ("xh", "z", "xl", "y", "c")
    )
    seq, ffn = ("xh", "z"), ("y", "c")
    rows = P(("xh", "z", "xl"), None)
    return jax.shard_map(
        on_device,
        mesh=fine,
        in_specs=(
            rows,
            rows,
            rows,
            rows,
            P("xl", None, ffn),
            P("xl", None, ffn),
            P("xl", ffn, None),
        ),
        out_specs=(
            P(("xh", "z", "xl"), ffn),
            P(("xh", "z", "xl"), ffn),
            P("xl", seq, ffn),
            P("xl", seq, ffn),
            P("xl", ffn, seq),
        ),
        check_vma=False,
    )
```

```python
import jax
import jax.numpy as jnp
from jax import lax
from jax.experimental import pallas as pl
from jax.experimental.pallas import tpu as pltpu
from jax.sharding import Mesh, PartitionSpec as P

CAP = 36
SLOT = 40
SOON = (0, 1, 7, 2, 6, 3)
LAST = (5, 4)
CUTS = 3
N_Z = 8
N_Y = 8
N_XL = 4
VMEM_BYTES = 20 * 1024 * 1024
BF16 = jnp.bfloat16
F32 = jnp.float32
HIGHEST = lax.Precision.HIGHEST


def dot(a, b, dims=((1,), (0,)), precision=None):
    return lax.dot_general(a, b, (dims, ((), ())), precision=precision, preferred_element_type=F32)


def picks(routes, gates, base=0):
    tok_count = routes.shape[1]
    shape = (N_XL * SLOT, tok_count)
    row = lax.broadcasted_iota(jnp.int32, shape, 0)
    expert = sum((row >= SLOT * i).astype(jnp.int32) for i in range(1, N_XL))
    slot = (row - SLOT * expert).astype(F32)
    expert = expert + base
    expert = jnp.where(expert >= N_XL, expert - N_XL, expert)
    first = routes[0:1, :] == expert
    second = routes[1:2, :] == expert
    member = jnp.where(first | second, 1.0, 0.0).astype(F32)
    at = lax.broadcasted_iota(jnp.int32, (tok_count, tok_count), 0)
    to = lax.broadcasted_iota(jnp.int32, (tok_count, tok_count), 1)
    earlier = jnp.where(at < to, 1.0, 0.0).astype(BF16)
    rank = dot(member.astype(BF16), earlier)
    pick = jnp.where(rank == slot, member, 0.0)
    gate = jnp.where(first, gates[0:1, :], gates[1:2, :]) * pick
    return pick, gate


def squeeze_matrix(rows, slots):
    row = lax.broadcasted_iota(jnp.int32, (rows, slots), 0)
    col = lax.broadcasted_iota(jnp.int32, (rows, slots), 1)
    expert = sum((row >= CAP * i).astype(jnp.int32) for i in range(1, N_XL))
    return jnp.where(col == row + (SLOT - CAP) * expert, 1.0, 0.0).astype(BF16)


def fetch_rows(pairs, sems):
    cuts = []
    for i, (a, b) in enumerate(pairs):
        step = a.shape[1] // CUTS
        at = [pl.ds(step * k, step) for k in range(CUTS)]
        cuts.append([pltpu.make_async_copy(a.at[:, r], b.at[:, r], sems.at[CUTS * i + k]) for k, r in enumerate(at)])
    for group in cuts:
        for copy in group:
            copy.start()
    return cuts


def fetch(pairs, sems):
    copies = [pltpu.make_async_copy(a, b, sems.at[i]) for i, (a, b) in enumerate(pairs)]
    for copy in copies:
        copy.start()
    return copies


def wait_all(copies):
    for copy in copies:
        copy.wait()


def dispatch(flags, routes_at, gates_at, tokens, cotangent, *refs):
    rows_out, (routes, gates, source, sem, sems) = refs[:N_XL], refs[N_XL:]
    is_x = flags[0] == 0
    copies = fetch(((routes_at, routes), (gates_at, gates)), sems)

    @pl.when(is_x)
    def _():
        pltpu.make_async_copy(tokens, source, sem).start()

    @pl.when(jnp.logical_not(is_x))
    def _():
        pltpu.make_async_copy(cotangent, source, sem).start()

    for copy in copies:
        copy.wait()
    pick, gate = picks(routes[...], gates[...], flags[3])
    scale = jnp.where(is_x, 1.0, jnp.sum(gate, axis=1, keepdims=True))
    pltpu.make_async_copy(tokens, source, sem).wait()
    rows = (dot(pick.astype(BF16), source[...]) * scale).astype(BF16)
    for k in range(N_XL):
        rows_out[k][...] = rows[SLOT * k : SLOT * (k + 1)]


def squeeze(flags, *refs):
    parts, (full_out, cols_out, cols, sems) = refs[:N_XL], refs[N_XL:]
    rows = jnp.concatenate([part[...] for part in parts], axis=0)
    matrix = squeeze_matrix(full_out.shape[0], rows.shape[0])
    full = dot(matrix, rows).astype(BF16)
    full_out[...] = full
    half = full.shape[1] // 2
    part = half // N_Z

    def write(swapped):
        for i in range(N_Z):
            low = full[:, part * i : part * (i + 1)]
            high = full[:, half + part * i : half + part * (i + 1)]
            cols[i] = jnp.concatenate([high, low] if swapped else [low, high], axis=1)

    @pl.when(flags[1] == 0)
    def _():
        write(False)

    @pl.when(flags[1] != 0)
    def _():
        write(True)

    wait_all(fetch([(cols.at[i], cols_out.at[i]) for i in range(N_Z)], sems))


def expert_front(flags, mine, other, gate_w, up_w, down_w, pieces_out, gate_v, up_v, down_v, sems):
    copies = fetch_rows(((gate_w, gate_v), (up_w, up_v), (down_w, down_v)), sems)
    is_x = flags[0] == 0
    a, b = mine[...], other[...]
    x = jnp.where(is_x, a, b)
    dy = jnp.where(is_x, b, a)
    wait_all(copies[0])
    gate_act = dot(x, gate_v[0], ((1,), (1,)))
    wait_all(copies[1])
    up_act = dot(x, up_v[0], ((1,), (1,)))
    wait_all(copies[2])
    hidden_grad = dot(dy, down_v[0], ((1,), (1,)))
    s = 1.0 / (1.0 + jnp.exp(-gate_act))
    silu = gate_act * s
    hidden = (silu * up_act).astype(BF16)
    gate_grad = (hidden_grad * up_act * s * (1.0 + gate_act * (1.0 - s))).astype(BF16)
    up_grad = (hidden_grad * silu).astype(BF16)
    pieces_out[...] = jnp.concatenate([hidden, gate_grad, up_grad], axis=1)


def expert_back(
    flags, pieces, gate_w, up_w, down_w, keep_out, send_out, gate_v, up_v, down_v, sems
):
    copies = fetch_rows(((down_w, down_v), (gate_w, gate_v), (up_w, up_v)), sems)
    ff = pieces.shape[1] // 3
    hidden = pieces[:, :ff]
    gate_grad = pieces[:, ff : 2 * ff]
    up_grad = pieces[:, 2 * ff :]
    wait_all(copies[0])
    out = dot(hidden, down_v[0]).astype(BF16)
    wait_all(copies[1])
    wait_all(copies[2])
    back = (dot(gate_grad, gate_v[0]) + dot(up_grad, up_v[0])).astype(BF16)
    part = out.shape[1] // (2 * N_Y)

    def write(even, odd):
        for i in range(N_Y):
            for j, ref in ((2 * i, even), (2 * i + 1, odd)):
                at = slice(part * j, part * (j + 1))
                ref[i] = jnp.concatenate([out[:, at], back[:, at]], axis=1)

    @pl.when(flags[0] == 0)
    def _():
        write(keep_out, send_out)

    @pl.when(flags[0] != 0)
    def _():
        write(send_out, keep_out)


def add_up(flags, blocks, rows_out):
    total = blocks[0].astype(F32)
    for i in range(1, N_Y):
        total = total + blocks[i].astype(F32)
    spread_out = squeeze_matrix(total.shape[0], N_XL * SLOT)
    rows = dot(spread_out, total.astype(BF16), ((0,), (0,))).astype(BF16)
    for k in range(N_XL):
        rows_out[lax.rem(flags[3] + (N_XL - k), N_XL)] = rows[SLOT * k : SLOT * (k + 1)]


def combine(routes, gates, rows, layer_out, grad_out):
    pick, gate = picks(routes[...], gates[...])
    part = layer_out.shape[1]
    both = rows[...]
    layer_out[...] = dot(gate, both[:, :part].astype(F32), ((0,), (0,)), HIGHEST).astype(BF16)
    grad_out[...] = dot(pick.astype(BF16), both[:, part:], ((0,), (0,))).astype(BF16)


def grads_of(flags, mine, other, distances, rows):
    is_x = flags[0] == 0
    order = [lax.rem(flags[2] + (N_Z - k), N_Z) for k in distances]
    a = jnp.concatenate([mine[k] for k in order], axis=0)
    b = jnp.concatenate([other[k] for k in order], axis=0)
    x = jnp.where(is_x, a, b)
    dy = jnp.where(is_x, b, a)
    ff = rows.shape[1] // 3
    down = dot(dy, rows[:, :ff], ((0,), (0,)))
    gate_up = dot(x, rows[:, ff:], ((0,), (0,)))
    return jnp.concatenate([down, gate_up], axis=1)


def weight_grads(flags, mine, other, *refs):
    *pieces, total_out, held, sems = refs
    count = pieces[0].shape[0]
    places = [held.at[pl.ds(count * i, count)] for i in range(len(SOON))]
    wait_all(fetch(list(zip(pieces, places)), sems))
    total_out[...] = grads_of(flags, mine, other, SOON, held[...])


def weight_grads_last(flags, mine, other, total, *refs):
    *pieces, keep_out, send_out = refs
    rows = jnp.concatenate([piece[...] for piece in pieces], axis=0)
    both = total[...] + grads_of(flags, mine, other, LAST, rows)
    part = keep_out.shape[0]
    keep_out[...] = both[:part]
    send_out[...] = both[part:].astype(BF16)


def finish(keep, got, gate_out, up_out, down_out):
    total = keep[...] + got[...].astype(F32)
    ff = total.shape[1] // 3
    down_out[0] = total[:, :ff]
    gate_out[0] = total[:, ff : 2 * ff]
    up_out[0] = total[:, 2 * ff :]


def call(body, outs, scalars, *operands, far=(), scratch=(), flops=0, far_outs=0):
    vmem = pl.BlockSpec(memory_space=pltpu.VMEM)
    smem = pl.BlockSpec(memory_space=pltpu.SMEM)
    hbm = pl.BlockSpec(memory_space=pltpu.HBM)
    moved = sum(v.size * v.dtype.itemsize for v in (*operands, *far))
    cost = pl.CostEstimate(flops=flops, transcendentals=0, bytes_accessed=moved)
    return pl.pallas_call(
        body,
        out_shape=[
            jax.ShapeDtypeStruct(s, t) if i < len(outs) - far_outs else pltpu.HBM(s, t)
            for i, (s, t) in enumerate(outs)
        ],
        in_specs=[smem] * len(scalars)
        + [vmem] * len(operands)
        + [hbm] * len(far),
        out_specs=[vmem] * (len(outs) - far_outs) + [hbm] * far_outs,
        scratch_shapes=list(scratch),
        compiler_params=pltpu.CompilerParams(vmem_limit_bytes=VMEM_BYTES),
        cost_estimate=cost if flops else None,
        name=body.__name__,
    )(*scalars, *operands, *[pltpu.with_memory_space_constraint(v, pltpu.HBM) for v in far])


def shift(value, by):
    return lax.ppermute(value, "z", [(i, (i + by) % N_Z) for i in range(N_Z)])


def spread(parts, axis, forward=1):
    count = len(parts)
    return [parts[0]] + [
        lax.ppermute(parts[k], axis, [(i, (i + forward * k) % count) for i in range(count)])
        for k in range(1, count)
    ]


def swap(value, axis):
    return lax.ppermute(value, axis, [(0, 1), (1, 0)])


def on_device(tokens, cotangent, routes, router_gates, gate_weight, up_weight, down_weight):
    width = tokens.shape[1]
    tok_count = tokens.shape[0]
    ff = gate_weight.shape[2]
    part = width // 16
    slots = N_XL * SLOT
    rows = N_XL * CAP
    work = 3 * 2 * rows * width * ff
    flags = jnp.stack([lax.axis_index(a) for a in ("c", "xh", "z", "xl", "y")]).astype(jnp.int32)
    routes = routes.T
    gates = router_gates.T
    weights = (jnp.swapaxes(gate_weight, 1, 2), jnp.swapaxes(up_weight, 1, 2), down_weight)
    held = [pltpu.VMEM(w.shape, BF16) for w in weights]
    held.append(pltpu.SemaphoreType.DMA((3 * CUTS,)))

    sent = call(
        dispatch,
        [((SLOT, width), BF16)] * N_XL,
        [flags],
        far=(routes, gates, tokens, cotangent),
        scratch=(
            pltpu.VMEM(routes.shape, routes.dtype),
            pltpu.VMEM(gates.shape, gates.dtype),
            pltpu.VMEM(tokens.shape, BF16),
            pltpu.SemaphoreType.DMA,
            pltpu.SemaphoreType.DMA((2,)),
        ),
    )
    got = spread(sent, "xl")
    mine, cols = call(
        squeeze,
        [((rows, width), BF16), ((N_Z, rows, 2 * part), BF16)],
        [flags],
        *got,
        scratch=(pltpu.VMEM((N_Z, rows, 2 * part), BF16), pltpu.SemaphoreType.DMA((N_Z,))),
        far_outs=1,
    )
    other = swap(mine, "c")
    cols = lax.all_to_all(cols, "z", split_axis=0, concat_axis=0, tiled=True)
    (pieces,) = call(
        expert_front, [((rows, 3 * ff), BF16)], [flags], mine, other, far=weights, scratch=held
    )
    keep, send = call(
        expert_back,
        [((N_Y, rows, 2 * part), BF16)] * 2,
        [flags],
        pieces,
        far=weights,
        scratch=held,
        flops=work,
    )
    summed = (keep.astype(F32) + swap(send, "c").astype(F32)).astype(BF16)

    found = [pieces] + [None] * (N_Z - 1)
    for k in range(1, N_Z // 2):
        found[k] = shift(found[k - 1], 1)
        found[N_Z - k] = shift(found[(N_Z - k + 1) % N_Z], -1)
    cols_other = swap(cols, "c")

    summed, _ = lax.optimization_barrier((summed, (found[1], found[7])))
    blocks = lax.all_to_all(summed, "y", split_axis=0, concat_axis=0, tiled=True)
    (back,) = call(add_up, [((N_XL, SLOT, 2 * part), BF16)], [flags], blocks)
    found[3], _ = lax.optimization_barrier((found[3], back))
    found[4] = shift(found[3], 1)
    back = lax.all_to_all(back, "xl", split_axis=0, concat_axis=0, tiled=True)
    layer_out, token_grad = call(
        combine,
        [((tok_count, part), BF16)] * 2,
        [],
        routes,
        gates,
        back.reshape(slots, 2 * part),
    )

    (total,) = call(
        weight_grads,
        [((2 * part, 3 * ff), F32)],
        [flags],
        cols,
        cols_other,
        far=[found[k] for k in SOON],
        scratch=(
            pltpu.VMEM((len(SOON) * rows, 3 * ff), BF16),
            pltpu.SemaphoreType.DMA((len(SOON),)),
        ),
        flops=2 * len(SOON) * rows * 2 * part * 3 * ff,
    )
    kept, given = call(
        weight_grads_last,
        [((part, 3 * ff), F32), ((part, 3 * ff), BF16)],
        [flags],
        cols,
        cols_other,
        total,
        *[found[k] for k in LAST],
    )
    given, _ = lax.optimization_barrier((given, back))
    received, layer_out, token_grad = lax.optimization_barrier(
        (swap(given, "xh"), layer_out, token_grad)
    )
    grad_gate, grad_up, grad_down = call(
        finish, [((1, part, ff), F32)] * 3, [], kept, received
    )
    return layer_out, token_grad, grad_gate, grad_up, jnp.swapaxes(grad_down, 1, 2)


def solution(mesh):
    fine = Mesh(
        mesh.devices.reshape(2, N_Z, N_XL, N_Y, 2), ("xh", "z", "xl", "y", "c")
    )
    seq, ffn = ("xh", "z"), ("y", "c")
    rows = P(("xh", "z", "xl"), None)
    return jax.shard_map(
        on_device,
        mesh=fine,
        in_specs=(
            rows,
            rows,
            rows,
            rows,
            P("xl", None, ffn),
            P("xl", None, ffn),
            P("xl", ffn, None),
        ),
        out_specs=(
            P(("xh", "z", "xl"), ffn),
            P(("xh", "z", "xl"), ffn),
            P("xl", seq, ffn),
            P("xl", seq, ffn),
            P("xl", ffn, seq),
        ),
        check_vma=False,
    )
```
